32 devices in a mesh: mode: 8 (over z, y), tile: 4 (over x, core).
Axes of the slice: x: 2, y: 2, z: 4, core: 2. Of those that a mesh axis runs over, the one named last changes fastest.
Arguments:
- magnetic: float32 [32, 6, 32, 512], P('mode', None, None, 'tile'), may hold values from -6 to 6
- velocity_stack: float32 [8, 9, 32, 512], P('mode', None, None, 'tile'), may hold values from -6 to 6
- wavenumber: int32 [32], P('mode'), may hold values from -16 to 15, as said below
- velocity_owner: int32 [1], replicated, may hold values from 0 to 7
Outputs:
- evolved: float32 [32, 6, 32, 512], P('mode', None, None, 'tile')
The draws below stay inside these ranges and needn't reach their ends.
Inputs may be any that keep to these rules, and one draw needn't show every extreme that they name: Slot k holds wavenumber ((k + s) mod 32) - 16 for one whole number s of the draw.
All inputs are finite; a program needn't handle non-finite values.
Results may differ from the reference program's by a relative error of at most 0.0003.
Values sent between devices are 32-bit elements; how exact they have to be, the bound alone decides.
No kernel may reach another device: no remote copies, remote signals or barrier semaphores. Data moves between devices by JAX's collectives and lax.ppermute only.
A program may use at most 64 MiB of HBM per device.

```python
import jax
import jax.numpy as jnp
from jax import lax

MODES = 32
ZW = 32
NR = 512
STEPS = 2
N_MODE = 8


def draw_wavenumber(key, part):
    offset = jax.random.randint(key, (), 0, MODES)
    slots = jnp.arange(MODES, dtype=jnp.int32)
    return ((slots + offset) % MODES - MODES // 2).astype(jnp.int32)


def levels(key, dims, shards, least, top_value):
    factor_of, own = 1.0, jax.random.fold_in(key, 6)
    for position, shards_of in shards:
        heights = jnp.exp(jax.random.uniform(jax.random.fold_in(own, position), (shards_of,), jnp.float32, least / len(shards), top_value / len(shards)))
        factor_of = factor_of * jnp.repeat(heights, dims[position] // shards_of).reshape([-1 if axis == position else 1 for axis in range(len(dims))])
    return factor_of


def noise(stream_key, shape, scale, reach, cuts=(), held_as=jnp.bfloat16):
    drawn = jax.random.normal(stream_key, shape, jnp.float32) * scale
    if len(cuts) > 0:
        drawn = levels(stream_key, shape, cuts, -0.22, 0.18) * drawn
    return jnp.clip(drawn, min=-reach, max=reach).astype(held_as)


def setup_inputs(seed: int = 0) -> dict:
    streams_of = jax.random.split(jax.random.key(seed), 5)
    magnetic = noise(streams_of[0], (MODES, 6, ZW, NR), 1.0, 6.0, ((0, 8), (3, 4)), jnp.float32)
    velocity_stack = noise(streams_of[1], (N_MODE, 9, ZW, NR), 1.0, 6.0, ((0, 8), (3, 4)), jnp.float32)
    wavenumber = draw_wavenumber(jax.random.fold_in(streams_of[4], 71), 0)
    velocity_owner = jax.random.randint(streams_of[3], (1,), 0, N_MODE).astype(jnp.int32)
    return dict(magnetic=magnetic, velocity_stack=velocity_stack, wavenumber=wavenumber, velocity_owner=velocity_owner)


diffusivity = 0.5
time_step = 0.2
inner_radius = 32.0


def complex_product(left_pair, right_pair):
    return (left_pair[0] * right_pair[0] - left_pair[1] * right_pair[1],
            left_pair[0] * right_pair[1] + left_pair[1] * right_pair[0])


def subtract_pair(left_pair, right_pair):
    return (left_pair[0] - right_pair[0], left_pair[1] - right_pair[1])


def components(values):
    return [(values[..., 2 * component, :, :], values[..., 2 * component + 1, :, :]) for component in range(3)]


def cross_product(left_vec, right_vec):
    radial_out = subtract_pair(complex_product(left_vec[1], right_vec[2]), complex_product(left_vec[2], right_vec[1]))
    azimuth_out = subtract_pair(complex_product(left_vec[2], right_vec[0]), complex_product(left_vec[0], right_vec[2]))
    axial_out = subtract_pair(complex_product(left_vec[0], right_vec[1]), complex_product(left_vec[1], right_vec[0]))
    return [radial_out, azimuth_out, axial_out]


def electromotive(velocity, lower_mode, centre, upper_mode):
    nothing = jnp.zeros_like(velocity[0])
    steady = [(velocity[0], nothing), (velocity[1], nothing), (velocity[2], nothing)]
    swirling = [(velocity[3], velocity[4]), (velocity[5], velocity[6]), (velocity[7], velocity[8])]
    mirror = [(pair[0], -pair[1]) for pair in swirling]
    first = cross_product(steady, components(centre))
    second = cross_product(swirling, components(lower_mode))
    third = cross_product(mirror, components(upper_mode))
    pieces = []
    for component in range(3):
        for part_index in range(2):
            pieces.append(first[component][part_index] + second[component][part_index] + third[component][part_index])
    return jnp.stack(pieces, axis=-3)


def interior(values):
    return values[..., 1:-1]


def pad_axial(values):
    return jnp.pad(values, [(0, 0)] * (values.ndim - 2) + [(1, 1), (0, 0)])


def along_axial(values):
    padded = pad_axial(values)
    return 0.5 * (padded[..., 2:, :] - padded[..., :-2, :])


def along_radial(values):
    return 0.5 * (values[..., 2:] - values[..., :-2])


def laplace(values, radius):
    centre = interior(values)
    padded = pad_axial(centre)
    return (values[..., 2:] + values[..., :-2] + padded[..., 2:, :] + padded[..., :-2, :]
            - 4.0 * centre + along_radial(values) / radius)


def radial_flux(values, radius):
    return 0.5 * ((radius + 1.0) * values[..., 2:] - (radius - 1.0) * values[..., :-2]) / radius


def rates(wide_field, wide_emf, waves, radius):
    field_r, field_p, field_z = components(wide_field)
    emf_r, emf_p, emf_z = components(wide_emf)
    wave_over = waves / radius
    decay_rate = (waves * waves + 1.0) / (radius * radius)
    coupling = 2.0 * waves / (radius * radius)
    axial_decay = waves * waves / (radius * radius)
    r_real = (-wave_over * interior(emf_z[1]) - along_axial(interior(emf_p[0]))
              + diffusivity * (laplace(field_r[0], radius) - decay_rate * interior(field_r[0]) + coupling * interior(field_p[1])))
    r_imag = (wave_over * interior(emf_z[0]) - along_axial(interior(emf_p[1]))
              + diffusivity * (laplace(field_r[1], radius) - decay_rate * interior(field_r[1]) - coupling * interior(field_p[0])))
    p_real = (along_axial(interior(emf_r[0])) - along_radial(emf_z[0])
              + diffusivity * (laplace(field_p[0], radius) - decay_rate * interior(field_p[0]) - coupling * interior(field_r[1])))
    p_imag = (along_axial(interior(emf_r[1])) - along_radial(emf_z[1])
              + diffusivity * (laplace(field_p[1], radius) - decay_rate * interior(field_p[1]) + coupling * interior(field_r[0])))
    z_real = (radial_flux(emf_p[0], radius) + wave_over * interior(emf_r[1])
              + diffusivity * (laplace(field_z[0], radius) - axial_decay * interior(field_z[0])))
    z_imag = (radial_flux(emf_p[1], radius) - wave_over * interior(emf_r[0])
              + diffusivity * (laplace(field_z[1], radius) - axial_decay * interior(field_z[1])))
    return jnp.stack([r_real, r_imag, p_real, p_imag, z_real, z_imag], axis=-3)


def evaluate(state, velocity, wavenumber, radius):
    modes_total = state.shape[0]

    def one_mode(slot):
        below = lax.dynamic_index_in_dim(state, ((slot - 1) % modes_total).astype(jnp.int32), 0, keepdims=False)
        centre = lax.dynamic_index_in_dim(state, slot, 0, keepdims=False)
        above = lax.dynamic_index_in_dim(state, ((slot + 1) % modes_total).astype(jnp.int32), 0, keepdims=False)
        emf = electromotive(velocity, below, centre, above)
        widths = ((0, 0), (0, 0), (1, 1))
        waves = lax.dynamic_index_in_dim(wavenumber, slot, 0, keepdims=False).astype(jnp.float32)
        return rates(jnp.pad(centre, widths), jnp.pad(emf, widths), waves, radius)

    return lax.map(one_mode, jnp.arange(modes_total, dtype=jnp.int32))


def reference(magnetic, velocity_stack, wavenumber, velocity_owner):
    velocity = lax.dynamic_index_in_dim(velocity_stack, velocity_owner[0].astype(jnp.int32), 0, keepdims=False)
    radius = inner_radius + jnp.arange(magnetic.shape[3], dtype=jnp.int32).astype(jnp.float32) + 0.5
    state = magnetic
    for step_index in range(STEPS):
        first = evaluate(state, velocity, wavenumber, radius)
        trial = state + time_step * first
        second = evaluate(trial, velocity, wavenumber, radius)
        state = state + (0.5 * time_step) * (first + second)
    return state
```

```python
import functools

import jax
import jax.numpy as jnp
from jax import lax
from jax.experimental import pallas as pl
from jax.experimental.pallas import tpu as pltpu
from jax.sharding import PartitionSpec as P

inner_radius = 32.0
f32 = jnp.float32
GROUP = 4
EDGE = 8
SLOTS = 3 * GROUP


def lane_index(rows=8):
    return lax.broadcasted_iota(jnp.int32, (rows, 128), 1)


def turn(x, shift, axis=1):
    if isinstance(shift, int):
        shift %= x.shape[axis]
        if shift == 0:
            return x
    return pltpu.roll(x, shift, axis)


def pack_kernel(field_ref, flow_ref, edges_ref):
    lane = lane_index()
    for comp in range(6):
        total = jnp.zeros((8, 128), f32)
        for zt in range(4):
            for mode in range(GROUP):
                at = 32 * zt + 8 * mode
                piece = turn(field_ref[mode, comp, 8 * zt : 8 * zt + 8, :], at + 4)
                total = jnp.where((lane >= at) & (lane < at + 8), piece, total)
        edges_ref[comp] = total
    for block in range(3):
        total = jnp.zeros((8, 128), f32)
        for part in range(4):
            row = 4 * block + part
            if row < 9:
                for zt in range(4):
                    at = 32 * part + 8 * zt
                    piece = turn(flow_ref[0, row, 8 * zt : 8 * zt + 8, :], at + 4)
                    total = jnp.where((lane >= at) & (lane < at + 8), piece, total)
        edges_ref[6 + block] = total


def join_kernel(pick_ref, edges_ref, left_ref, right_ref, left2_ref, right2_ref, flow_ref, flow2_ref, strips_ref, message_ref):
    low = lane_index() % 8 < 4
    for comp in range(6):
        strips_ref[0, comp] = jnp.where(low, left_ref[comp], edges_ref[comp])
        strips_ref[1, comp] = jnp.where(low, edges_ref[comp], right_ref[comp])
    keep = pick_ref[0] == 0

    @pl.when(keep)
    def _():
        for row in range(9):
            message_ref[32 * row : 32 * row + 32, :] = flow_ref[0, row]
        for block in range(3):
            message_ref[288 + 8 * block : 296 + 8 * block, :] = jnp.where(low, left_ref[6 + block], right_ref[6 + block])

    @pl.when(jnp.logical_not(keep))
    def _():
        for row in range(9):
            message_ref[32 * row : 32 * row + 32, :] = flow2_ref[0, row]
        for block in range(3):
            message_ref[288 + 8 * block : 296 + 8 * block, :] = jnp.where(low, left2_ref[block], right2_ref[block])


def emf_of(flow, lower, centre, upper):
    total = [lower[i] + upper[i] for i in range(6)]
    gap = [lower[i] - upper[i] for i in range(6)]
    steady = flow[0:3]
    swirl_re = (flow[3], flow[5], flow[7])
    swirl_im = (flow[4], flow[6], flow[8])
    out = []
    for comp in range(3):
        i, j = (comp + 1) % 3, (comp + 2) % 3
        real = (
            (steady[i] * centre[2 * j] - steady[j] * centre[2 * i])
            + (swirl_re[i] * total[2 * j] - swirl_re[j] * total[2 * i])
            - (swirl_im[i] * gap[2 * j + 1] - swirl_im[j] * gap[2 * i + 1])
        )
        imag = (
            (steady[i] * centre[2 * j + 1] - steady[j] * centre[2 * i + 1])
            + (swirl_re[i] * total[2 * j + 1] - swirl_re[j] * total[2 * i + 1])
            + (swirl_im[i] * gap[2 * j] - swirl_im[j] * gap[2 * i])
        )
        out += [real, imag]
    return out


def coefficients(radius):
    inner, outer = radius - 1.0, radius + 1.0
    return dict(
        up=1.0 + 0.5 / inner, down=1.0 - 0.5 / outer, flux_up=radius / inner, flux_down=radius / outer,
        inv=1.0 / radius, inv2=1.0 / (radius * radius),
    )


def stencil(field, emf, coef, waves):
    decay = -4.0 - (waves * waves + 1.0) * coef["inv2"]
    axial_decay = -4.0 - (waves * waves) * coef["inv2"]
    coupling = (2.0 * waves) * coef["inv2"]
    wave_over = (2.0 * waves) * coef["inv"]
    up, down = coef["up"], coef["down"]
    right = [field[i] * up for i in range(6)]
    left = [field[i] * down for i in range(6)]
    above = list(field)
    below = list(field)
    place = [field[i] * (decay if i < 4 else axial_decay) for i in range(6)]
    for part in range(2):
        right[2 + part] = right[2 + part] - emf[4 + part]
        left[2 + part] = left[2 + part] + emf[4 + part]
        right[4 + part] = right[4 + part] + emf[2 + part] * coef["flux_up"]
        left[4 + part] = left[4 + part] - emf[2 + part] * coef["flux_down"]
        above[part] = field[part] - emf[2 + part]
        below[part] = field[part] + emf[2 + part]
        above[2 + part] = field[2 + part] + emf[part]
        below[2 + part] = field[2 + part] - emf[part]
    place[0] = place[0] + coupling * field[3] - wave_over * emf[5]
    place[1] = place[1] - coupling * field[2] + wave_over * emf[4]
    place[2] = place[2] - coupling * field[1]
    place[3] = place[3] + coupling * field[0]
    place[4] = place[4] + wave_over * emf[1]
    place[5] = place[5] - wave_over * emf[0]
    return right, left, above, below, place


def steps_kernel(
    modes, tiles, info_ref, flow_ref, flow2_ref, strips_own, strips_low, strips_high, own_hbm, low_hbm, high_hbm, out_ref,
    state, trial, half, strip, strip_trial, strip_half, inject, flow, flow_strip, sems,
):
    loads = [
        pltpu.make_async_copy(src, state.at[pl.ds(GROUP * i, GROUP)], sems.at[i])
        for i, src in enumerate((low_hbm, own_hbm, high_hbm))
    ]
    for load in loads:
        load.start()
    base, tile, take = info_ref[0], info_ref[1], info_ref[2]
    lane8, lane = lane_index(), lane_index(32)
    row = lax.broadcasted_iota(jnp.int32, (32, 128), 0)
    column8 = lane8 % 8

    for source, wanted in ((flow_ref, 0), (flow2_ref, 1)):

        @pl.when(take == wanted)
        def _(source=source):
            for r in range(9):
                flow[r] = source[32 * r : 32 * r + 32, :]
            own = jnp.where(column8 < 4, 124 + column8, column8 - 4)
            for r in range(9):
                halo = source[288 + 8 * (r // 4) : 296 + 8 * (r // 4), :]
                for zt in range(4):
                    rows = slice(8 * zt, 8 * zt + 8)
                    inside = jnp.take_along_axis(source[32 * r + 8 * zt : 32 * r + 8 * zt + 8, :], own, axis=1)
                    outside = jnp.take_along_axis(halo, 32 * (r % 4) + 8 * zt + column8, axis=1)
                    flow_strip[0, r, rows] = jnp.where(column8 < 4, outside, inside)
                    flow_strip[1, r, rows] = jnp.where(column8 < 4, inside, outside)

    for side in range(2):
        for comp in range(6):
            low, own, high = strips_low[side, comp], strips_own[side, comp], strips_high[side, comp]
            for zt in range(4):
                value = jnp.where(lane8 < 32, turn(low, -32 * zt), turn(own, 32 - 32 * zt))
                value = jnp.where(lane8 < 64, value, turn(high, 64 - 32 * zt))
                strip[side, comp, 8 * zt : 8 * zt + 8] = jnp.where(lane8 < 96, value, 0.0)

    def wave_at(slot):
        return lax.rem(base + slot, modes) - modes // 2

    first_column = tile * 128
    radius = inner_radius + 0.5 + (first_column + lane8[:1]).astype(f32)
    main_coef = coefficients(radius)
    strip_waves = wave_at(lane8[:1] // 8).astype(f32)
    strip_coef, strip_inside = [], []
    for side in range(2):
        column = first_column + column8[:1] + (124 if side else -4)
        strip_coef.append(coefficients(inner_radius + 0.5 + column.astype(f32)))
        strip_inside.append((column >= 0) & (column < tiles * 128))

    def from_above(x):
        return turn(jnp.where(row == 0, 0.0, x), -1, 0)

    def from_below(x):
        return turn(jnp.where(row == 31, 0.0, x), 1, 0)

    def strips_eval(source, store):
        rights = []
        for side in range(2):
            centre = [source[side, i] for i in range(6)]
            lower = [turn(x, EDGE) for x in centre]
            upper = [turn(x, -EDGE) for x in centre]
            emf = emf_of([flow_strip[side, r] for r in range(9)], lower, centre, upper)
            right, left, above, below, place = stencil(centre, emf, strip_coef[side], strip_waves)
            if side == 0:
                for i in range(6):
                    inject[i] = left[i]
            else:
                for i in range(6):
                    inject[i] = jnp.where(lane % 8 == 4, right[i], inject[i])
            if store is not None:
                for i in range(6):
                    twice = (turn(right[i], -1) + turn(left[i], 1)) + (from_above(above[i]) + from_below(below[i])) + place[i]
                    store(side, i, jnp.where(strip_inside[side], twice, 0.0), centre[i])

    def main_eval(source, start, stop, store):
        def one(k, carry):
            waves = wave_at(k).astype(f32)
            centre = [source[k, i] for i in range(6)]
            emf = emf_of(
                [flow[r] for r in range(9)], [source[k - 1, i] for i in range(6)], centre, [source[k + 1, i] for i in range(6)]
            )
            right, left, above, below, place = stencil(centre, emf, main_coef, waves)
            away = 124 - EDGE * k
            for i in range(6):
                edge = pltpu.roll(inject[i], away, 1)
                next_column = turn(jnp.where(lane == 0, edge, right[i]), -1)
                last_column = turn(jnp.where(lane == 127, edge, left[i]), 1)
                twice = (next_column + last_column) + (from_above(above[i]) + from_below(below[i])) + place[i]
                store(k, i, twice, centre[i])
            return carry

        lax.fori_loop(start, stop, one, 0)

    def first_main(k, i, twice, value):
        trial[k, i] = value + 0.1 * twice
        half[k, i] = value + 0.05 * twice

    def second_main(k, i, twice, value):
        state[k, i] = half[k, i] + 0.05 * twice

    def last_main(k, i, twice, value):
        out_ref[k - GROUP, i] = half[k, i] + 0.05 * twice

    def first_strip(side, i, twice, value):
        strip_trial[side, i] = value + 0.1 * twice
        strip_half[side, i] = value + 0.05 * twice

    def second_strip(side, i, twice, value):
        strip[side, i] = strip_half[side, i] + 0.05 * twice

    strips_eval(strip, first_strip)
    for load in loads:
        load.wait()
    main_eval(state, 1, 11, first_main)
    strips_eval(strip_trial, second_strip)
    main_eval(trial, 2, 10, second_main)
    strips_eval(strip, first_strip)
    main_eval(state, 3, 9, first_main)
    strips_eval(strip_trial, None)
    main_eval(trial, 4, 8, last_main)


VMEM = pl.BlockSpec(memory_space=pltpu.VMEM)
SMEM = pl.BlockSpec(memory_space=pltpu.SMEM)
ANY = pl.BlockSpec(memory_space=pl.ANY)


def shape(*dims):
    return jax.ShapeDtypeStruct(dims, f32)


def body(magnetic, velocity_stack, wavenumber, velocity_owner):
    groups, tiles = lax.axis_size("mode"), lax.axis_size("tile")
    me, tile = lax.axis_index("mode"), lax.axis_index("tile")
    modes = groups * GROUP
    away = jnp.bitwise_xor(me, velocity_owner[0])

    def to_mode(x, step):
        return lax.ppermute(x, "mode", [(i, (i + step) % groups) for i in range(groups)])

    def across(x, bit):
        return lax.ppermute(x, "mode", [(i, i ^ bit) for i in range(groups)])

    def to_tile(x, step):
        return lax.ppermute(x, "tile", [(i, i + step) for i in range(tiles) if 0 <= i + step < tiles])

    def to_tile_across(x, step, bit):
        pairs = [
            (g * tiles + i, (g ^ bit) * tiles + i + step)
            for g in range(groups)
            for i in range(tiles)
            if 0 <= i + step < tiles
        ]
        return lax.ppermute(x, ("mode", "tile"), pairs)

    flow2 = across(velocity_stack, 1)
    low = to_mode(magnetic, 1)
    high = to_mode(magnetic, -1)
    edges = pl.pallas_call(pack_kernel, out_shape=shape(9, 8, 128), in_specs=[VMEM, VMEM], out_specs=VMEM, name="pack_edges")(
        magnetic, velocity_stack
    )
    left, right = to_tile(edges, 1), to_tile(edges, -1)
    left2, right2 = to_tile_across(edges[6:], 1, 1), to_tile_across(edges[6:], -1, 1)
    strips, message = pl.pallas_call(
        join_kernel,
        out_shape=(shape(2, 6, 8, 128), shape(312, 128)),
        in_specs=[SMEM] + [VMEM] * 7,
        out_specs=(VMEM, VMEM),
        name="join_edges",
    )(jnp.bitwise_and(away, 1).reshape(1), edges, left, right, left2, right2, velocity_stack, flow2)
    strips_low, strips_high = to_mode(strips, 1), to_mode(strips, -1)
    bit = 2
    while 2 * bit < groups:
        message = jnp.where(jnp.bitwise_and(away, bit) == 0, message, across(message, bit))
        bit *= 2
    message2 = across(message, bit)
    info = jnp.stack(
        [
            lax.rem(wavenumber[0] + modes // 2 + modes - GROUP, modes),
            tile,
            (jnp.bitwise_and(away, bit) != 0).astype(jnp.int32),
        ]
    ).astype(jnp.int32)
    return pl.pallas_call(
        functools.partial(steps_kernel, modes, tiles),
        out_shape=shape(GROUP, 6, 32, 128),
        in_specs=[SMEM] + [VMEM] * 5 + [ANY] * 3,
        out_specs=VMEM,
        scratch_shapes=[
            pltpu.VMEM((SLOTS, 6, 32, 128), f32),
            pltpu.VMEM((SLOTS, 6, 32, 128), f32),
            pltpu.VMEM((SLOTS, 6, 32, 128), f32),
            pltpu.VMEM((2, 6, 32, 128), f32),
            pltpu.VMEM((2, 6, 32, 128), f32),
            pltpu.VMEM((2, 6, 32, 128), f32),
            pltpu.VMEM((6, 32, 128), f32),
            pltpu.VMEM((9, 32, 128), f32),
            pltpu.VMEM((2, 9, 32, 128), f32),
            pltpu.SemaphoreType.DMA((3,)),
        ],
        compiler_params=pltpu.CompilerParams(vmem_limit_bytes=32 * 1024 * 1024),
        name="heun_steps",
    )(info, message, message2, strips, strips_low, strips_high, magnetic, low, high)


def solution(mesh):
    placed = (P("mode", None, None, "tile"), P("mode", None, None, "tile"), P("mode"), P())
    return jax.shard_map(
        body, mesh=mesh, in_specs=placed, out_specs=P("mode", None, None, "tile"), check_vma=False
    )
```

```python
import functools

import jax
import jax.numpy as jnp
from jax import lax
from jax.experimental import pallas as pl
from jax.experimental.pallas import tpu as pltpu
from jax.sharding import PartitionSpec as P

inner_radius = 32.0
f32 = jnp.float32
GROUP = 4
EDGE = 8
SLOTS = 3 * GROUP


def lane_index(rows=8):
    return lax.broadcasted_iota(jnp.int32, (rows, 128), 1)


def turn(x, shift, axis=1):
    if isinstance(shift, int):
        shift %= x.shape[axis]
        if shift == 0:
            return x
    return pltpu.roll(x, shift, axis)


def pack_kernel(field_ref, flow_ref, edges_ref):
    lane = lane_index()
    for comp in range(6):
        total = jnp.zeros((8, 128), f32)
        for zt in range(4):
            for mode in range(GROUP):
                at = 32 * zt + 8 * mode
                piece = turn(field_ref[mode, comp, 8 * zt : 8 * zt + 8, :], at + 4)
                total = jnp.where((lane >= at) & (lane < at + 8), piece, total)
        edges_ref[comp] = total
    for block in range(3):
        total = jnp.zeros((8, 128), f32)
        for part in range(4):
            row = 4 * block + part
            if row < 9:
                for zt in range(4):
                    at = 32 * part + 8 * zt
                    piece = turn(flow_ref[0, row, 8 * zt : 8 * zt + 8, :], at + 4)
                    total = jnp.where((lane >= at) & (lane < at + 8), piece, total)
        edges_ref[6 + block] = total


def strips_kernel(edges_ref, left_ref, right_ref, strips_ref, halo_ref):
    low = lane_index() % 8 < 4
    for comp in range(6):
        strips_ref[0, comp] = jnp.where(low, left_ref[comp], edges_ref[comp])
        strips_ref[1, comp] = jnp.where(low, edges_ref[comp], right_ref[comp])
    for block in range(3):
        halo_ref[block] = jnp.where(low, left_ref[6 + block], right_ref[6 + block])


def join_kernel(pick_ref, flow_ref, flow2_ref, halo_ref, halo2_ref, strips_ref, message_ref):
    for side in range(2):
        for comp in range(6):
            at = 312 + 48 * side + 8 * comp
            message_ref[at : at + 8, :] = strips_ref[side, comp]
    for source, halo, wanted in ((flow_ref, halo_ref, 0), (flow2_ref, halo2_ref, 1)):

        @pl.when(jnp.where(pick_ref[0] == 0, 0, 1) == wanted)
        def _(source=source, halo=halo):
            for row in range(9):
                message_ref[32 * row : 32 * row + 32, :] = source[0, row]
            for block in range(3):
                message_ref[288 + 8 * block : 296 + 8 * block, :] = halo[block]


def emf_of(flow, lower, centre, upper):
    total = [lower[i] + upper[i] for i in range(6)]
    gap = [lower[i] - upper[i] for i in range(6)]
    steady = flow[0:3]
    swirl_re = (flow[3], flow[5], flow[7])
    swirl_im = (flow[4], flow[6], flow[8])
    out = []
    for comp in range(3):
        i, j = (comp + 1) % 3, (comp + 2) % 3
        real = (
            (steady[i] * centre[2 * j] - steady[j] * centre[2 * i])
            + (swirl_re[i] * total[2 * j] - swirl_re[j] * total[2 * i])
            - (swirl_im[i] * gap[2 * j + 1] - swirl_im[j] * gap[2 * i + 1])
        )
        imag = (
            (steady[i] * centre[2 * j + 1] - steady[j] * centre[2 * i + 1])
            + (swirl_re[i] * total[2 * j + 1] - swirl_re[j] * total[2 * i + 1])
            + (swirl_im[i] * gap[2 * j] - swirl_im[j] * gap[2 * i])
        )
        out += [real, imag]
    return out


def coefficients(radius):
    inner, outer = radius - 1.0, radius + 1.0
    return dict(
        up=1.0 + 0.5 / inner, down=1.0 - 0.5 / outer, flux_up=radius / inner, flux_down=radius / outer,
        inv=1.0 / radius, inv2=1.0 / (radius * radius),
    )


def stencil(field, emf, coef, waves):
    decay = -4.0 - (waves * waves + 1.0) * coef["inv2"]
    axial_decay = -4.0 - (waves * waves) * coef["inv2"]
    coupling = (2.0 * waves) * coef["inv2"]
    wave_over = (2.0 * waves) * coef["inv"]
    up, down = coef["up"], coef["down"]
    right = [field[i] * up for i in range(6)]
    left = [field[i] * down for i in range(6)]
    above = list(field)
    below = list(field)
    place = [field[i] * (decay if i < 4 else axial_decay) for i in range(6)]
    for part in range(2):
        right[2 + part] = right[2 + part] - emf[4 + part]
        left[2 + part] = left[2 + part] + emf[4 + part]
        right[4 + part] = right[4 + part] + emf[2 + part] * coef["flux_up"]
        left[4 + part] = left[4 + part] - emf[2 + part] * coef["flux_down"]
        above[part] = field[part] - emf[2 + part]
        below[part] = field[part] + emf[2 + part]
        above[2 + part] = field[2 + part] + emf[part]
        below[2 + part] = field[2 + part] - emf[part]
    place[0] = place[0] + coupling * field[3] - wave_over * emf[5]
    place[1] = place[1] - coupling * field[2] + wave_over * emf[4]
    place[2] = place[2] - coupling * field[1]
    place[3] = place[3] + coupling * field[0]
    place[4] = place[4] + wave_over * emf[1]
    place[5] = place[5] - wave_over * emf[0]
    return right, left, above, below, place


def start_loads(info_ref, own_hbm, pair_hbm, other_hbm, state, sems):
    odd = info_ref[3]
    places = (GROUP, 2 * GROUP * (1 - odd), 2 * GROUP * odd)
    loads = [
        pltpu.make_async_copy(src, state.at[pl.ds(place, GROUP)], sems.at[i])
        for i, (src, place) in enumerate(zip((own_hbm, pair_hbm, other_hbm), places))
    ]
    for load in loads:
        load.start()
    return loads


def wave_at(base, slot, modes):
    return (lax.rem(base + slot, modes) - modes // 2).astype(f32)


def column_radius(column):
    return inner_radius + 0.5 + column.astype(f32)


def from_above(x):
    row = lax.broadcasted_iota(jnp.int32, (32, 128), 0)
    return turn(jnp.where(row == 0, 0.0, x), -1, 0)


def from_below(x):
    row = lax.broadcasted_iota(jnp.int32, (32, 128), 0)
    return turn(jnp.where(row == 31, 0.0, x), 1, 0)


def main_eval(source, flow, coef, base, modes, start, stop, edges, store):
    lane = lane_index(32)

    def one(k, carry):
        centre = [source[k, i] for i in range(6)]
        emf = emf_of(
            [flow[r] for r in range(9)], [source[k - 1, i] for i in range(6)], centre, [source[k + 1, i] for i in range(6)]
        )
        right, left, above, below, place = stencil(centre, emf, coef, wave_at(base, k, modes))
        for i in range(6):
            edge = pltpu.roll(edges[i], 124 - EDGE * k, 1)
            next_column = turn(jnp.where(lane == 0, edge, right[i]), -1)
            last_column = turn(jnp.where(lane == 127, edge, left[i]), 1)
            twice = (next_column + last_column) + (from_above(above[i]) + from_below(below[i])) + place[i]
            store(k, i, twice, centre[i])
        return carry

    lax.fori_loop(start, stop, one, 0)


def steps_kernel(
    modes, tiles, info_ref, message_ref, message2_ref, strips_own, strips_other, own_hbm, pair_hbm, other_hbm,
    out_ref, state, trial, half, strip, strip_trial, strip_half, inject, flow, flow_strip, sems,
):
    loads = start_loads(info_ref, own_hbm, pair_hbm, other_hbm, state, sems)
    base, tile, take, odd = info_ref[0], info_ref[1], info_ref[2], info_ref[3]
    lane8, lane = lane_index(), lane_index(32)
    column8 = lane8 % 8

    for source, wanted in ((message_ref, 0), (message2_ref, 1)):

        @pl.when(take == wanted)
        def _(source=source):
            for r in range(9):
                flow[r] = source[32 * r : 32 * r + 32, :]
            near = jnp.where(column8 < 4, 124 + column8, column8 - 4)
            for r in range(9):
                halo = source[288 + 8 * (r // 4) : 296 + 8 * (r // 4), :]
                for zt in range(4):
                    rows = slice(8 * zt, 8 * zt + 8)
                    inside = jnp.take_along_axis(source[32 * r + 8 * zt : 32 * r + 8 * zt + 8, :], near, axis=1)
                    outside = jnp.take_along_axis(halo, 32 * (r % 4) + 8 * zt + column8, axis=1)
                    flow_strip[0, r, rows] = jnp.where(column8 < 4, outside, inside)
                    flow_strip[1, r, rows] = jnp.where(column8 < 4, inside, outside)

    for side in range(2):
        for comp in range(6):
            at = 312 + 48 * side + 8 * comp
            own, other, pair = strips_own[side, comp], strips_other[side, comp], message2_ref[at : at + 8, :]
            low, high = jnp.where(odd == 1, pair, other), jnp.where(odd == 1, other, pair)
            for zt in range(4):
                value = jnp.where(lane8 < 32, turn(low, -32 * zt), turn(own, 32 - 32 * zt))
                value = jnp.where(lane8 < 64, value, turn(high, 64 - 32 * zt))
                strip[side, comp, 8 * zt : 8 * zt + 8] = jnp.where(lane8 < 96, value, 0.0)

    first_column = tile * 128
    main_coef = coefficients(column_radius(first_column + lane8[:1]))
    strip_waves = wave_at(base, lane8[:1] // 8, modes)
    strip_coef, strip_inside = [], []
    for side in range(2):
        column = first_column + column8[:1] + (124 if side else -4)
        strip_coef.append(coefficients(column_radius(column)))
        strip_inside.append((column >= 0) & (column < tiles * 128))

    def strips_eval(source, store):
        for side in range(2):
            centre = [source[side, i] for i in range(6)]
            lower = [turn(x, EDGE) for x in centre]
            upper = [turn(x, -EDGE) for x in centre]
            emf = emf_of([flow_strip[side, r] for r in range(9)], lower, centre, upper)
            right, left, above, below, place = stencil(centre, emf, strip_coef[side], strip_waves)
            for i in range(6):
                inject[i] = jnp.where(lane % 8 == 4, right[i], inject[i]) if side else left[i]
                if store is not None:
                    twice = (turn(right[i], -1) + turn(left[i], 1)) + (from_above(above[i]) + from_below(below[i])) + place[i]
                    store(side, i, jnp.where(strip_inside[side], twice, 0.0), centre[i])

    def first_main(k, i, twice, value):
        trial[k, i] = value + 0.1 * twice
        half[k, i] = value + 0.05 * twice

    def second_main(k, i, twice, value):
        state[k, i] = half[k, i] + 0.05 * twice

    def last_main(k, i, twice, value):
        out_ref[k - GROUP, i] = half[k, i] + 0.05 * twice

    def first_strip(side, i, twice, value):
        strip_trial[side, i] = value + 0.1 * twice
        strip_half[side, i] = value + 0.05 * twice

    def second_strip(side, i, twice, value):
        strip[side, i] = strip_half[side, i] + 0.05 * twice

    main = functools.partial(main_eval, flow=flow, coef=main_coef, base=base, modes=modes, edges=inject)
    strips_eval(strip, first_strip)
    for load in loads:
        load.wait()
    main(state, start=1, stop=11, store=first_main)
    strips_eval(strip_trial, second_strip)
    main(trial, start=2, stop=10, store=second_main)
    strips_eval(strip, first_strip)
    main(state, start=3, stop=9, store=first_main)
    strips_eval(strip_trial, None)
    main(trial, start=4, stop=8, store=last_main)


VMEM = pl.BlockSpec(memory_space=pltpu.VMEM)
SMEM = pl.BlockSpec(memory_space=pltpu.SMEM)
ANY = pl.BlockSpec(memory_space=pl.ANY)


SMALL = pl.CostEstimate(flops=8, bytes_accessed=8, transcendentals=0)


def shape(*dims):
    return jax.ShapeDtypeStruct(dims, f32)


def small_kernel(kernel, name, out, in_specs):
    out_specs = (VMEM,) * len(out) if isinstance(out, tuple) else VMEM
    return pl.pallas_call(kernel, out_shape=out, in_specs=in_specs, out_specs=out_specs, cost_estimate=SMALL, name=name)


def body(magnetic, velocity_stack, wavenumber, velocity_owner):
    groups, tiles = lax.axis_size("mode"), lax.axis_size("tile")
    me, tile = lax.axis_index("mode"), lax.axis_index("tile")
    modes = groups * GROUP
    away = jnp.bitwise_xor(me, velocity_owner[0])

    def to_pair(x, first):
        pairs = []
        for i in range(first, groups, 2):
            pairs += [(i, (i + 1) % groups), ((i + 1) % groups, i)]
        return lax.ppermute(x, "mode", pairs)

    def across(x, bit):
        return lax.ppermute(x, "mode", [(i, i ^ bit) for i in range(groups)])

    def to_tile(x, step):
        return lax.ppermute(x, "tile", [(i, i + step) for i in range(tiles) if 0 <= i + step < tiles])

    bits = []
    while 2 << len(bits) < groups:
        bits.append(2 << len(bits))
    bits.append(1)
    def choose(x, y, bit):
        return jnp.where(jnp.bitwise_and(away, bit) == 0, x, y)

    pair = to_pair(magnetic, 0)
    flow = choose(velocity_stack, across(velocity_stack, bits[0]), bits[0])
    magnetic_later, flow = lax.optimization_barrier((magnetic, flow))
    other = to_pair(magnetic_later, 1)

    def small_exchanges(flow, magnetic):
        for bit in bits[1:-2]:
            flow = choose(flow, across(flow, bit), bit)
        flow2 = across(flow, bits[-2])
        edges = small_kernel(pack_kernel, "pack_edges", shape(9, 8, 128), [VMEM] * 2)(magnetic, flow)
        strips, halo = small_kernel(strips_kernel, "strips", (shape(2, 6, 8, 128), shape(3, 8, 128)), [VMEM] * 3)(
            edges, to_tile(edges, 1), to_tile(edges, -1)
        )
        halo2 = across(halo, bits[-2])
        pick = jnp.bitwise_and(away, bits[-2]).reshape(1)
        message = small_kernel(join_kernel, "join", shape(408, 128), [SMEM] + [VMEM] * 5)(
            pick, flow, flow2, halo, halo2, strips
        )
        return message, across(message, bits[-1]), strips, to_pair(strips, 1)

    def none(flow, magnetic):
        message, strips = jnp.zeros((408, 128), f32), jnp.zeros((2, 6, 8, 128), f32)
        return message, message, strips, strips

    message, message2, strips, strips_other = lax.cond(velocity_owner[0] >= 0, small_exchanges, none, flow, magnetic)
    info = jnp.stack(
        [
            lax.rem(wavenumber[0] + modes // 2 + modes - GROUP, modes),
            tile,
            jnp.bitwise_and(away, bits[-1]),
            jnp.bitwise_and(me, 1),
        ]
    ).astype(jnp.int32)
    return pl.pallas_call(
        functools.partial(steps_kernel, modes, tiles),
        out_shape=shape(GROUP, 6, 32, 128),
        in_specs=[SMEM] + [VMEM] * 4 + [ANY] * 3,
        out_specs=VMEM,
        scratch_shapes=[
            pltpu.VMEM((SLOTS, 6, 32, 128), f32),
            pltpu.VMEM((SLOTS, 6, 32, 128), f32),
            pltpu.VMEM((SLOTS, 6, 32, 128), f32),
            pltpu.VMEM((2, 6, 32, 128), f32),
            pltpu.VMEM((2, 6, 32, 128), f32),
            pltpu.VMEM((2, 6, 32, 128), f32),
            pltpu.VMEM((6, 32, 128), f32),
            pltpu.VMEM((9, 32, 128), f32),
            pltpu.VMEM((2, 9, 32, 128), f32),
            pltpu.SemaphoreType.DMA((3,)),
        ],
        compiler_params=pltpu.CompilerParams(vmem_limit_bytes=32 * 1024 * 1024),
        name="heun_steps",
    )(info, message, message2, strips, strips_other, magnetic, pair, other)


def solution(mesh):
    placed = (P("mode", None, None, "tile"), P("mode", None, None, "tile"), P("mode"), P())
    return jax.shard_map(
        body, mesh=mesh, in_specs=placed, out_specs=P("mode", None, None, "tile"), check_vma=False
    )
```

```python
import functools

import jax
import jax.numpy as jnp
from jax import lax
from jax.experimental import pallas as pl
from jax.experimental.pallas import tpu as pltpu
from jax.sharding import PartitionSpec as P

inner_radius = 32.0
f32 = jnp.float32
GROUP = 4
EDGE = 8
SLOTS = 3 * GROUP


def lane_index(rows=8):
    return lax.broadcasted_iota(jnp.int32, (rows, 128), 1)


def turn(x, shift, axis=1):
    if isinstance(shift, int):
        shift %= x.shape[axis]
        if shift == 0:
            return x
    return pltpu.roll(x, shift, axis)


def pack_kernel(field_ref, flow_ref, edges_ref):
    lane = lane_index()
    for comp in range(6):
        total = jnp.zeros((8, 128), f32)
        for zt in range(4):
            for mode in range(GROUP):
                at = 32 * zt + 8 * mode
                piece = turn(field_ref[mode, comp, 8 * zt : 8 * zt + 8, :], at + 4)
                total = jnp.where((lane >= at) & (lane < at + 8), piece, total)
        edges_ref[comp] = total
    for block in range(3):
        total = jnp.zeros((8, 128), f32)
        for part in range(4):
            row = 4 * block + part
            if row < 9:
                for zt in range(4):
                    at = 32 * part + 8 * zt
                    piece = turn(flow_ref[0, row, 8 * zt : 8 * zt + 8, :], at + 4)
                    total = jnp.where((lane >= at) & (lane < at + 8), piece, total)
        edges_ref[6 + block] = total


def strips_kernel(place_ref, edges_ref, near_ref, far_ref, strips_ref, halo_ref):
    low = lane_index() % 8 < 4
    odd = place_ref[0] % 2 == 1
    for row in range(9):
        left = jnp.where(odd, near_ref[row], far_ref[row])
        right = jnp.where(odd, far_ref[row], near_ref[row])
        if row < 6:
            strips_ref[0, row] = jnp.where(low, left, edges_ref[row])
            strips_ref[1, row] = jnp.where(low, edges_ref[row], right)
        else:
            halo_ref[row - 6] = jnp.where(low, left, right)


def join_kernel(pick_ref, halo_ref, halo2_ref, strips_ref, message_ref):
    other = pick_ref[0] != 0
    for block in range(3):
        message_ref[block] = jnp.where(other, halo2_ref[block], halo_ref[block])
    for side in range(2):
        for comp in range(6):
            message_ref[3 + 6 * side + comp] = strips_ref[side, comp]


def emf_of(flow, centre, total, gap):
    steady = flow[0:3]
    swirl_re = (flow[3], flow[5], flow[7])
    swirl_im = (flow[4], flow[6], flow[8])
    out = []
    for comp in range(3):
        i, j = (comp + 1) % 3, (comp + 2) % 3
        real = (
            (steady[i] * centre[2 * j] - steady[j] * centre[2 * i])
            + (swirl_re[i] * total[2 * j] - swirl_re[j] * total[2 * i])
            - (swirl_im[i] * gap[2 * j + 1] - swirl_im[j] * gap[2 * i + 1])
        )
        imag = (
            (steady[i] * centre[2 * j + 1] - steady[j] * centre[2 * i + 1])
            + (swirl_re[i] * total[2 * j + 1] - swirl_re[j] * total[2 * i + 1])
            + (swirl_im[i] * gap[2 * j] - swirl_im[j] * gap[2 * i])
        )
        out += [real, imag]
    return out


def coefficients(radius):
    inner, outer = radius - 1.0, radius + 1.0
    return dict(
        up=1.0 + 0.5 / inner, down=1.0 - 0.5 / outer, flux_up=radius / inner, flux_down=radius / outer,
        inv=1.0 / radius, inv2=1.0 / (radius * radius),
    )


def with_waves(coef, waves):
    return dict(
        coef, waves=waves, decay=6.0 - (waves * waves + 1.0) * coef["inv2"], axial=6.0 - (waves * waves) * coef["inv2"],
        coupling=(2.0 * waves) * coef["inv2"], over=(2.0 * waves) * coef["inv"],
    )


def stencil(field, emf, coef):
    up, down, decay, axial, coupling, over = (coef[n] for n in ("up", "down", "decay", "axial", "coupling", "over"))
    right = [field[i] * up for i in range(6)]
    left = [field[i] * down for i in range(6)]
    place = [field[i] * (decay if i < 4 else axial) for i in range(6)]
    for part in range(2):
        right[2 + part] = right[2 + part] - emf[4 + part]
        left[2 + part] = left[2 + part] + emf[4 + part]
        right[4 + part] = right[4 + part] + emf[2 + part] * coef["flux_up"]
        left[4 + part] = left[4 + part] - emf[2 + part] * coef["flux_down"]
    place[0] = place[0] + (coupling * field[3] - over * emf[5])
    place[1] = place[1] - (coupling * field[2] - over * emf[4])
    place[2] = place[2] - coupling * field[1]
    place[3] = place[3] + coupling * field[0]
    place[4] = place[4] + over * emf[1]
    place[5] = place[5] - over * emf[0]
    return right, left, place


PAD = 8


def tile_rows(zt, shift=0):
    return pl.ds(PAD + 8 * zt + shift, 8)


def add_rows(total, i, get_field, get_emf):
    total = total + (get_field(i, 1) + get_field(i, -1))
    if i < 2:
        total = total - (get_emf(2 + i, 1) - get_emf(2 + i, -1))
    elif i < 4:
        total = total + (get_emf(i - 2, 1) - get_emf(i - 2, -1))
    return total


def wave_at(base, slot, modes):
    return (lax.rem(base + slot, modes) - modes // 2).astype(f32)


def column_radius(column):
    return inner_radius + 0.5 + column.astype(f32)


def steps_kernel(
    modes, tiles, info_ref, flow_hbm, flow2_hbm, message_hbm, message2_hbm, strips_hbm, own_hbm, pair_hbm, other_hbm, out_hbm,
    state, trial, out, strip, strip_trial, inject, flow, flow_strip, near_message, far_message, other_strips, emfs, emfs_strip, sums, gaps, rights, lefts, sems,
):
    base, tile, take, odd = info_ref[0], info_ref[1], info_ref[2], info_ref[3]

    places = (GROUP, 2 * GROUP * (1 - odd), 2 * GROUP * odd)
    rows = pl.ds(PAD, 32)
    loads = [
        pltpu.make_async_copy(message_hbm, near_message, sems.at[0]),
        pltpu.make_async_copy(message2_hbm, far_message, sems.at[1]),
        pltpu.make_async_copy(strips_hbm, other_strips, sems.at[2]),
    ]
    field_loads = [
        pltpu.make_async_copy(src, state.at[pl.ds(place, GROUP), :, rows], sems.at[4 + i])
        for i, (src, place) in enumerate(zip((own_hbm, pair_hbm, other_hbm), places))
    ]
    for load in loads:
        load.start()

    @pl.when(take == 0)
    def _():
        pltpu.make_async_copy(flow_hbm.at[0], flow, sems.at[3]).start()

    @pl.when(take != 0)
    def _():
        pltpu.make_async_copy(flow2_hbm.at[0], flow, sems.at[3]).start()

    for load in field_loads:
        load.start()

    lane8 = lane_index()
    column8 = lane8 % 8
    zeros = jnp.zeros((8, 128), f32)
    for array in (state, trial):

        def clear(k, carry, array=array):
            for i in range(6):
                array[k, i, 0:PAD, :] = zeros
                array[k, i, PAD + 32 : PAD + 40, :] = zeros
            return carry

        lax.fori_loop(0, SLOTS, clear, 0)
    for array in (strip, strip_trial, emfs_strip, emfs):
        for side in range(2):
            for i in range(array.shape[1]):
                array[side, i, 0:PAD, :] = zeros
                array[side, i, PAD + 32 : PAD + 40, :] = zeros

    first_column = tile * 128
    main_coef = coefficients(column_radius(first_column + lane8))
    strip_coef, strip_inside = [], []
    for side in range(2):
        column = first_column + column8 + (124 if side else -4)
        strip_coef.append(with_waves(coefficients(column_radius(column)), wave_at(base, lane8 // 8, modes)))
        strip_inside.append((column >= 0) & (column < tiles * 128))

    for load in loads:
        load.wait()
    for side in range(2):
        for comp in range(6):
            at = 3 + 6 * side + comp
            own, other, pair = near_message[at], other_strips[side, comp], far_message[at]
            low, high = jnp.where(odd == 1, pair, other), jnp.where(odd == 1, other, pair)
            for zt in range(4):
                value = jnp.where(lane8 < 32, turn(low, -32 * zt), turn(own, 32 - 32 * zt))
                value = jnp.where(lane8 < 64, value, turn(high, 64 - 32 * zt))
                strip[side, comp, tile_rows(zt), :] = jnp.where(lane8 < 96, value, 0.0)

    pltpu.make_async_copy(flow_hbm.at[0], flow, sems.at[3]).wait()
    near = jnp.where(column8 < 4, 124 + column8, column8 - 4)
    for r in range(9):
        halo = jnp.where(take == 0, near_message[r // 4], far_message[r // 4])
        for zt in range(4):
            inside = jnp.take_along_axis(flow[r, 8 * zt : 8 * zt + 8, :], near, axis=1)
            outside = jnp.take_along_axis(halo, 32 * (r % 4) + 8 * zt + column8, axis=1)
            flow_strip[0, r, 8 * zt : 8 * zt + 8, :] = jnp.where(column8 < 4, outside, inside)
            flow_strip[1, r, 8 * zt : 8 * zt + 8, :] = jnp.where(column8 < 4, inside, outside)

    def strips_eval(source, store):
        places = [(side, zt) for side in range(2) for zt in range(4)]
        for side, zt in places:
            at = slice(8 * zt, 8 * zt + 8)
            for i in range(6):
                x = source[side, i, tile_rows(zt), :]
                lower, upper = turn(x, EDGE), turn(x, -EDGE)
                sums[side, i, at], gaps[side, i, at] = lower + upper, lower - upper
        terms = {}
        for side, zt in places:
            at = slice(8 * zt, 8 * zt + 8)
            centre = [source[side, i, tile_rows(zt), :] for i in range(6)]
            velocity = [flow_strip[side, r, at, :] for r in range(9)]
            emf = emf_of(velocity, centre, [sums[side, i, at] for i in range(6)], [gaps[side, i, at] for i in range(6)])
            right, left, terms[side, zt] = stencil(centre, emf, strip_coef[side])
            for i in range(4):
                emfs_strip[side, i, tile_rows(zt), :] = emf[i]
            for i in range(6):
                rights[side, i, at], lefts[side, i, at] = right[i], left[i]
        for side, zt in places:
            at = slice(8 * zt, 8 * zt + 8)
            for i in range(6):
                if store is not None or side:
                    next_column = turn(rights[side, i, at], -1)
                if store is not None or not side:
                    last_column = turn(lefts[side, i, at], 1)
                inject[i, at] = jnp.where(column8 == 3, next_column, inject[i, at]) if side else last_column
                if store is not None:
                    total = add_rows(
                        (next_column + last_column) + terms[side, zt][i], i,
                        lambda c, d: source[side, c, tile_rows(zt, d), :],
                        lambda c, d: emfs_strip[side, c, tile_rows(zt, d), :],
                    )
                    store(side, i, zt, jnp.where(strip_inside[side], total, 0.0))

    def main_eval(source, start, stop, store, after=None):
        def one(k, buffer):
            coef = with_waves(main_coef, wave_at(base, k, modes))
            totals = []
            for zt in range(4):
                centre = [source[k, i, tile_rows(zt), :] for i in range(6)]
                lower = [source[k - 1, i, tile_rows(zt), :] for i in range(6)]
                upper = [source[k + 1, i, tile_rows(zt), :] for i in range(6)]
                total = [lower[i] + upper[i] for i in range(6)]
                gap = [lower[i] - upper[i] for i in range(6)]
                emf = emf_of([flow[r, 8 * zt : 8 * zt + 8, :] for r in range(9)], centre, total, gap)
                for i in range(4):
                    emfs[buffer, i, tile_rows(zt), :] = emf[i]
                right, left, place = stencil(centre, emf, coef)
                total = []
                for i in range(6):
                    edge = pltpu.roll(inject[i, 8 * zt : 8 * zt + 8, :], 124 - EDGE * k, 1)
                    next_column = jnp.where(lane8 == 127, edge, turn(right[i], -1))
                    last_column = jnp.where(lane8 == 0, edge, turn(left[i], 1))
                    total.append((next_column + last_column) + place[i])
                totals.append(total)
            for zt in range(4):
                for i in range(6):
                    total = add_rows(
                        totals[zt][i], i,
                        lambda c, d: source[k, c, tile_rows(zt, d), :],
                        lambda c, d: emfs[buffer, c, tile_rows(zt, d), :],
                    )
                    store(k, i, zt, total)

        def two(n, carry):
            one(start + 2 * n, 0)
            one(start + 2 * n + 1, 1)
            if after is not None:
                after(n)
            return carry

        lax.fori_loop(0, (stop - start) // 2, two, 0)

    def first_main(k, i, zt, total):
        trial[k, i, tile_rows(zt), :] = total

    def second_main(k, i, zt, total):
        state[k, i, tile_rows(zt), :] = 0.5 * state[k, i, tile_rows(zt), :] + 0.005 * total

    def last_main(k, i, zt, total):
        out[k - GROUP, i, 8 * zt : 8 * zt + 8, :] = 0.5 * state[k, i, tile_rows(zt), :] + 0.005 * total

    def first_strip(side, i, zt, total):
        strip_trial[side, i, tile_rows(zt), :] = total

    def second_strip(side, i, zt, total):
        strip[side, i, tile_rows(zt), :] = 0.5 * strip[side, i, tile_rows(zt), :] + 0.005 * total

    strips_eval(strip, first_strip)
    for load in field_loads:
        load.wait()
    main_eval(state, 1, 11, first_main)
    strips_eval(strip_trial, second_strip)
    main_eval(trial, 2, 10, second_main)
    strips_eval(strip, first_strip)
    main_eval(state, 3, 9, first_main)
    strips_eval(strip_trial, None)
    def writing(n):
        done = pl.ds(2 * n, 2)
        return pltpu.make_async_copy(out.at[done], out_hbm.at[done], sems.at[n])

    main_eval(trial, 4, 8, last_main, lambda n: writing(n).start())
    for n in range(GROUP // 2):
        writing(n).wait()


VMEM = pl.BlockSpec(memory_space=pltpu.VMEM)
SMEM = pl.BlockSpec(memory_space=pltpu.SMEM)
ANY = pl.BlockSpec(memory_space=pl.ANY)


SMALL = pl.CostEstimate(flops=8, bytes_accessed=8, transcendentals=0)


def shape(*dims):
    return jax.ShapeDtypeStruct(dims, f32)


def small_kernel(kernel, name, out, in_specs):
    out_specs = (VMEM,) * len(out) if isinstance(out, tuple) else VMEM
    return pl.pallas_call(kernel, out_shape=out, in_specs=in_specs, out_specs=out_specs, cost_estimate=SMALL, name=name)


def steps_call(kernel):
    return pl.pallas_call(
        kernel,
        out_shape=shape(GROUP, 6, 32, 128),
        in_specs=[SMEM] + [ANY] * 8,
        out_specs=ANY,
        scratch_shapes=[
            pltpu.VMEM((SLOTS, 6, 48, 128), f32),
            pltpu.VMEM((SLOTS, 6, 48, 128), f32),
            pltpu.VMEM((GROUP, 6, 32, 128), f32),
            pltpu.VMEM((2, 6, 48, 128), f32),
            pltpu.VMEM((2, 6, 48, 128), f32),
            pltpu.VMEM((6, 32, 128), f32),
            pltpu.VMEM((9, 32, 128), f32),
            pltpu.VMEM((2, 9, 32, 128), f32),
            pltpu.VMEM((15, 8, 128), f32),
            pltpu.VMEM((15, 8, 128), f32),
            pltpu.VMEM((2, 6, 8, 128), f32),
            pltpu.VMEM((2, 4, 48, 128), f32),
            pltpu.VMEM((2, 4, 48, 128), f32),
            pltpu.VMEM((2, 6, 32, 128), f32),
            pltpu.VMEM((2, 6, 32, 128), f32),
            pltpu.VMEM((2, 6, 32, 128), f32),
            pltpu.VMEM((2, 6, 32, 128), f32),
            pltpu.SemaphoreType.DMA((8,)),
        ],
        compiler_params=pltpu.CompilerParams(vmem_limit_bytes=32 * 1024 * 1024),
        name="heun_steps",
    )


def body(magnetic, velocity_stack, wavenumber, velocity_owner):
    groups, tiles = lax.axis_size("mode"), lax.axis_size("tile")
    me, tile = lax.axis_index("mode"), lax.axis_index("tile")
    modes = groups * GROUP
    away = jnp.bitwise_xor(me, velocity_owner[0])

    def to_pair(x, first):
        pairs = []
        for i in range(first, groups, 2):
            pairs += [(i, (i + 1) % groups), ((i + 1) % groups, i)]
        return lax.ppermute(x, "mode", pairs)

    def across(x, bit):
        return lax.ppermute(x, "mode", [(i, i ^ bit) for i in range(groups)])

    def to_tile(x, first):
        pairs = []
        for i in range(first, tiles - 1, 2):
            pairs += [(i, i + 1), (i + 1, i)]
        return lax.ppermute(x, "tile", pairs)

    bits = []
    while 2 << len(bits) < groups:
        bits.append(2 << len(bits))
    bits.append(1)
    def choose(x, y, bit):
        return jnp.where(jnp.bitwise_and(away, bit) == 0, x, y)

    pair = to_pair(magnetic, 0)
    flow = choose(velocity_stack, across(velocity_stack, bits[0]), bits[0])
    magnetic_later, flow = lax.optimization_barrier((magnetic, flow))
    other = to_pair(magnetic_later, 1)

    def small_exchanges(flow, magnetic):
        for bit in bits[1:-2]:
            flow = choose(flow, across(flow, bit), bit)
        flow2 = across(flow, bits[-2])
        edges = small_kernel(pack_kernel, "pack_edges", shape(9, 8, 128), [VMEM] * 2)(magnetic, flow)
        strips, halo = small_kernel(
            strips_kernel, "strips", (shape(2, 6, 8, 128), shape(3, 8, 128)), [SMEM] + [VMEM] * 3
        )(tile.reshape(1), edges, to_tile(edges, 0), to_tile(edges, 1))
        halo2 = across(halo, bits[-2])
        flow, flow2, halo, halo2 = lax.optimization_barrier((flow, flow2, halo, halo2))
        pick = jnp.bitwise_and(away, bits[-2]).reshape(1)
        message = small_kernel(join_kernel, "join", shape(15, 8, 128), [SMEM] + [VMEM] * 3)(pick, halo, halo2, strips)
        flow = choose(flow, flow2, bits[-2])
        return flow, across(flow, bits[-1]), message, across(message, bits[-1]), to_pair(strips, 1)

    def none(flow, magnetic):
        message, strips = jnp.zeros((15, 8, 128), f32), jnp.zeros((2, 6, 8, 128), f32)
        return flow, flow, message, message, strips

    *flows, strips_other = lax.cond(velocity_owner[0] >= 0, small_exchanges, none, flow, magnetic)
    info = jnp.stack(
        [
            lax.rem(wavenumber[0] + modes // 2 + modes - GROUP, modes),
            tile,
            jnp.bitwise_and(away, bits[-1]),
            jnp.bitwise_and(me, 1),
        ]
    ).astype(jnp.int32)
    return steps_call(functools.partial(steps_kernel, modes, tiles))(info, *flows, strips_other, magnetic, pair, other)


def solution(mesh):
    placed = (P("mode", None, None, "tile"), P("mode", None, None, "tile"), P("mode"), P())
    return jax.shard_map(
        body, mesh=mesh, in_specs=placed, out_specs=P("mode", None, None, "tile"), check_vma=False
    )
```

```python
import functools

import jax
import jax.numpy as jnp
from jax import lax
from jax.experimental import pallas as pl
from jax.experimental.pallas import tpu as pltpu
from jax.sharding import PartitionSpec as P

inner_radius = 32.0
f32 = jnp.float32
GROUP = 4
EDGE = 8
SLOTS = 3 * GROUP


def lane_index(rows=8):
    return lax.broadcasted_iota(jnp.int32, (rows, 128), 1)


def turn(x, shift, axis=1):
    if isinstance(shift, int):
        shift %= x.shape[axis]
        if shift == 0:
            return x
    return pltpu.roll(x, shift, axis)


def pack_kernel(field_ref, flow_ref, edges_ref):
    lane = lane_index()
    for comp in range(6):
        total = jnp.zeros((8, 128), f32)
        for zt in range(4):
            for mode in range(GROUP):
                at = 32 * zt + 8 * mode
                piece = turn(field_ref[mode, comp, 8 * zt : 8 * zt + 8, :], at + 4)
                total = jnp.where((lane >= at) & (lane < at + 8), piece, total)
        edges_ref[comp] = total
    for block in range(3):
        total = jnp.zeros((8, 128), f32)
        for part in range(4):
            row = 4 * block + part
            if row < 9:
                for zt in range(4):
                    at = 32 * part + 8 * zt
                    piece = turn(flow_ref[0, row, 8 * zt : 8 * zt + 8, :], at + 4)
                    total = jnp.where((lane >= at) & (lane < at + 8), piece, total)
        edges_ref[6 + block] = total


def strips_kernel(place_ref, edges_ref, near_ref, far_ref, strips_ref, halo_ref):
    low = lane_index() % 8 < 4
    odd = place_ref[0] % 2 == 1
    for row in range(9):
        left = jnp.where(odd, near_ref[row], far_ref[row])
        right = jnp.where(odd, far_ref[row], near_ref[row])
        if row < 6:
            strips_ref[0, row] = jnp.where(low, left, edges_ref[row])
            strips_ref[1, row] = jnp.where(low, edges_ref[row], right)
        else:
            halo_ref[row - 6] = jnp.where(low, left, right)


def join_kernel(pick_ref, halo_ref, halo2_ref, strips_ref, message_ref):
    other = pick_ref[0] != 0
    for block in range(3):
        message_ref[block] = jnp.where(other, halo2_ref[block], halo_ref[block])
    for side in range(2):
        for comp in range(6):
            message_ref[3 + 6 * side + comp] = strips_ref[side, comp]


def emf_of(flow, centre, total, gap):
    steady = flow[0:3]
    swirl_re = (flow[3], flow[5], flow[7])
    swirl_im = (flow[4], flow[6], flow[8])
    out = []
    for comp in range(3):
        i, j = (comp + 1) % 3, (comp + 2) % 3
        real = (
            (steady[i] * centre[2 * j] - steady[j] * centre[2 * i])
            + (swirl_re[i] * total[2 * j] - swirl_re[j] * total[2 * i])
            - (swirl_im[i] * gap[2 * j + 1] - swirl_im[j] * gap[2 * i + 1])
        )
        imag = (
            (steady[i] * centre[2 * j + 1] - steady[j] * centre[2 * i + 1])
            + (swirl_re[i] * total[2 * j + 1] - swirl_re[j] * total[2 * i + 1])
            + (swirl_im[i] * gap[2 * j] - swirl_im[j] * gap[2 * i])
        )
        out += [real, imag]
    return out


def coefficients(radius):
    inner, outer = radius - 1.0, radius + 1.0
    return dict(
        up=1.0 + 0.5 / inner, down=1.0 - 0.5 / outer, flux_up=radius / inner, flux_down=radius / outer,
        inv=1.0 / radius, inv2=1.0 / (radius * radius),
    )


def with_waves(coef, waves):
    return dict(
        coef, waves=waves, decay=6.0 - (waves * waves + 1.0) * coef["inv2"], axial=6.0 - (waves * waves) * coef["inv2"],
        coupling=(2.0 * waves) * coef["inv2"], over=(2.0 * waves) * coef["inv"],
    )


def stencil(field, emf, coef):
    up, down, decay, axial, coupling, over = (coef[n] for n in ("up", "down", "decay", "axial", "coupling", "over"))
    right = [field[i] * up for i in range(6)]
    left = [field[i] * down for i in range(6)]
    place = [field[i] * (decay if i < 4 else axial) for i in range(6)]
    for part in range(2):
        right[2 + part] = right[2 + part] - emf[4 + part]
        left[2 + part] = left[2 + part] + emf[4 + part]
        right[4 + part] = right[4 + part] + emf[2 + part] * coef["flux_up"]
        left[4 + part] = left[4 + part] - emf[2 + part] * coef["flux_down"]
    place[0] = place[0] + (coupling * field[3] - over * emf[5])
    place[1] = place[1] - (coupling * field[2] - over * emf[4])
    place[2] = place[2] - coupling * field[1]
    place[3] = place[3] + coupling * field[0]
    place[4] = place[4] + over * emf[1]
    place[5] = place[5] - over * emf[0]
    return right, left, place


PAD = 8


def tile_rows(zt, shift=0):
    return pl.ds(PAD + 8 * zt + shift, 8)


def add_rows(total, i, get_field, get_emf):
    total = total + (get_field(i, 1) + get_field(i, -1))
    if i < 2:
        total = total - (get_emf(2 + i, 1) - get_emf(2 + i, -1))
    elif i < 4:
        total = total + (get_emf(i - 2, 1) - get_emf(i - 2, -1))
    return total


def wave_at(base, slot, modes):
    return (lax.rem(base + slot, modes) - modes // 2).astype(f32)


def column_radius(column):
    return inner_radius + 0.5 + column.astype(f32)


def steps_kernel(
    modes, tiles, info_ref, flow_hbm, flow2_hbm, message_hbm, message2_hbm, strips_hbm, own_hbm, pair_hbm, other_hbm, out_hbm,
    state, trial, out, strip, strip_trial, inject, flow, flow_strip, near_message, far_message, other_strips, emfs, emfs_strip, sums, gaps, rights, lefts, sems,
):
    base, tile, take, odd = info_ref[0], info_ref[1], info_ref[2], info_ref[3]

    places = (GROUP, 2 * GROUP * (1 - odd), 2 * GROUP * odd)
    rows = pl.ds(PAD, 32)
    loads = [
        pltpu.make_async_copy(message_hbm, near_message, sems.at[0]),
        pltpu.make_async_copy(message2_hbm, far_message, sems.at[1]),
        pltpu.make_async_copy(strips_hbm, other_strips, sems.at[2]),
    ]
    field_loads = [
        pltpu.make_async_copy(src, state.at[pl.ds(place, GROUP), :, rows], sems.at[4 + i])
        for i, (src, place) in enumerate(zip((own_hbm, pair_hbm, other_hbm), places))
    ]
    for load in loads:
        load.start()

    @pl.when(take == 0)
    def _():
        pltpu.make_async_copy(flow_hbm.at[0], flow, sems.at[3]).start()

    @pl.when(take != 0)
    def _():
        pltpu.make_async_copy(flow2_hbm.at[0], flow, sems.at[3]).start()

    for load in field_loads:
        load.start()

    lane8 = lane_index()
    column8 = lane8 % 8
    zeros = jnp.zeros((8, 128), f32)
    for array in (state, trial):

        def clear(k, carry, array=array):
            for i in range(6):
                array[k, i, 0:PAD, :] = zeros
                array[k, i, PAD + 32 : PAD + 40, :] = zeros
            return carry

        lax.fori_loop(0, SLOTS, clear, 0)
    for array in (strip, strip_trial, emfs_strip, emfs):
        for side in range(2):
            for i in range(array.shape[1]):
                array[side, i, 0:PAD, :] = zeros
                array[side, i, PAD + 32 : PAD + 40, :] = zeros

    first_column = tile * 128
    main_coef = coefficients(column_radius(first_column + lane8))
    strip_coef, strip_inside = [], []
    for side in range(2):
        column = first_column + column8 + (124 if side else -4)
        strip_coef.append(with_waves(coefficients(column_radius(column)), wave_at(base, lane8 // 8, modes)))
        strip_inside.append((column >= 0) & (column < tiles * 128))

    for load in loads:
        load.wait()
    for side in range(2):
        for comp in range(6):
            at = 3 + 6 * side + comp
            own, other, pair = near_message[at], other_strips[side, comp], far_message[at]
            low, high = jnp.where(odd == 1, pair, other), jnp.where(odd == 1, other, pair)
            for zt in range(4):
                value = jnp.where(lane8 < 32, turn(low, -32 * zt), turn(own, 32 - 32 * zt))
                value = jnp.where(lane8 < 64, value, turn(high, 64 - 32 * zt))
                strip[side, comp, tile_rows(zt), :] = jnp.where(lane8 < 96, value, 0.0)

    pltpu.make_async_copy(flow_hbm.at[0], flow, sems.at[3]).wait()
    near = jnp.where(column8 < 4, 124 + column8, column8 - 4)
    for r in range(9):
        halo = jnp.where(take == 0, near_message[r // 4], far_message[r // 4])
        for zt in range(4):
            inside = jnp.take_along_axis(flow[r, 8 * zt : 8 * zt + 8, :], near, axis=1)
            outside = jnp.take_along_axis(halo, 32 * (r % 4) + 8 * zt + column8, axis=1)
            flow_strip[0, r, 8 * zt : 8 * zt + 8, :] = jnp.where(column8 < 4, outside, inside)
            flow_strip[1, r, 8 * zt : 8 * zt + 8, :] = jnp.where(column8 < 4, inside, outside)

    def strips_eval(source, store):
        places = [(side, zt) for side in range(2) for zt in range(4)]
        for side, zt in places:
            at = slice(8 * zt, 8 * zt + 8)
            for i in range(6):
                x = source[side, i, tile_rows(zt), :]
                lower, upper = turn(x, EDGE), turn(x, -EDGE)
                sums[side, i, at], gaps[side, i, at] = lower + upper, lower - upper
        terms = {}
        for side, zt in places:
            at = slice(8 * zt, 8 * zt + 8)
            centre = [source[side, i, tile_rows(zt), :] for i in range(6)]
            velocity = [flow_strip[side, r, at, :] for r in range(9)]
            emf = emf_of(velocity, centre, [sums[side, i, at] for i in range(6)], [gaps[side, i, at] for i in range(6)])
            right, left, terms[side, zt] = stencil(centre, emf, strip_coef[side])
            for i in range(4):
                emfs_strip[side, i, tile_rows(zt), :] = emf[i]
            for i in range(6):
                rights[side, i, at], lefts[side, i, at] = right[i], left[i]
        for side, zt in places:
            at = slice(8 * zt, 8 * zt + 8)
            for i in range(6):
                if store is not None or side:
                    next_column = turn(rights[side, i, at], -1)
                if store is not None or not side:
                    last_column = turn(lefts[side, i, at], 1)
                inject[i, at] = jnp.where(column8 == 3, next_column, inject[i, at]) if side else last_column
                if store is not None:
                    total = add_rows(
                        (next_column + last_column) + terms[side, zt][i], i,
                        lambda c, d: source[side, c, tile_rows(zt, d), :],
                        lambda c, d: emfs_strip[side, c, tile_rows(zt, d), :],
                    )
                    store(side, i, zt, jnp.where(strip_inside[side], total, 0.0))

    def main_eval(source, start, stop, store, after=None):
        def one(k, buffer):
            coef = with_waves(main_coef, wave_at(base, k, modes))
            totals = []
            for zt in range(4):
                centre = [source[k, i, tile_rows(zt), :] for i in range(6)]
                lower = [source[k - 1, i, tile_rows(zt), :] for i in range(6)]
                upper = [source[k + 1, i, tile_rows(zt), :] for i in range(6)]
                total = [lower[i] + upper[i] for i in range(6)]
                gap = [lower[i] - upper[i] for i in range(6)]
                emf = emf_of([flow[r, 8 * zt : 8 * zt + 8, :] for r in range(9)], centre, total, gap)
                for i in range(4):
                    emfs[buffer, i, tile_rows(zt), :] = emf[i]
                right, left, place = stencil(centre, emf, coef)
                total = []
                for i in range(6):
                    edge = pltpu.roll(inject[i, 8 * zt : 8 * zt + 8, :], 124 - EDGE * k, 1)
                    next_column = jnp.where(lane8 == 127, edge, turn(right[i], -1))
                    last_column = jnp.where(lane8 == 0, edge, turn(left[i], 1))
                    total.append((next_column + last_column) + place[i])
                totals.append(total)
            for zt in range(4):
                for i in range(6):
                    total = add_rows(
                        totals[zt][i], i,
                        lambda c, d: source[k, c, tile_rows(zt, d), :],
                        lambda c, d: emfs[buffer, c, tile_rows(zt, d), :],
                    )
                    store(k, i, zt, total)

        def two(n, carry):
            one(start + 2 * n, 0)
            one(start + 2 * n + 1, 1)
            if after is not None:
                after(n)
            return carry

        lax.fori_loop(0, (stop - start) // 2, two, 0)

    def first_main(k, i, zt, total):
        trial[k, i, tile_rows(zt), :] = total

    def second_main(k, i, zt, total):
        state[k, i, tile_rows(zt), :] = 0.5 * state[k, i, tile_rows(zt), :] + 0.005 * total

    def last_main(k, i, zt, total):
        out[k - GROUP, i, 8 * zt : 8 * zt + 8, :] = 0.5 * state[k, i, tile_rows(zt), :] + 0.005 * total

    def first_strip(side, i, zt, total):
        strip_trial[side, i, tile_rows(zt), :] = total

    def second_strip(side, i, zt, total):
        strip[side, i, tile_rows(zt), :] = 0.5 * strip[side, i, tile_rows(zt), :] + 0.005 * total

    strips_eval(strip, first_strip)
    for load in field_loads:
        load.wait()
    main_eval(state, 1, 11, first_main)
    strips_eval(strip_trial, second_strip)
    main_eval(trial, 2, 10, second_main)
    strips_eval(strip, first_strip)
    main_eval(state, 3, 9, first_main)
    strips_eval(strip_trial, None)
    def writing(n):
        done = pl.ds(2 * n, 2)
        return pltpu.make_async_copy(out.at[done], out_hbm.at[done], sems.at[n])

    main_eval(trial, 4, 8, last_main, lambda n: writing(n).start())
    for n in range(GROUP // 2):
        writing(n).wait()


VMEM = pl.BlockSpec(memory_space=pltpu.VMEM)
SMEM = pl.BlockSpec(memory_space=pltpu.SMEM)
ANY = pl.BlockSpec(memory_space=pl.ANY)


SMALL = pl.CostEstimate(flops=8, bytes_accessed=8, transcendentals=0)
LONG = pl.CostEstimate(flops=1_000_000_000, bytes_accessed=100_000_000, transcendentals=0)


def shape(*dims):
    return jax.ShapeDtypeStruct(dims, f32)


def small_kernel(kernel, name, out, in_specs, cost=SMALL):
    out_specs = (VMEM,) * len(out) if isinstance(out, tuple) else VMEM
    return pl.pallas_call(kernel, out_shape=out, in_specs=in_specs, out_specs=out_specs, cost_estimate=cost, name=name)


def steps_call(kernel):
    return pl.pallas_call(
        kernel,
        out_shape=shape(GROUP, 6, 32, 128),
        in_specs=[SMEM] + [ANY] * 8,
        out_specs=ANY,
        scratch_shapes=[
            pltpu.VMEM((SLOTS, 6, 48, 128), f32),
            pltpu.VMEM((SLOTS, 6, 48, 128), f32),
            pltpu.VMEM((GROUP, 6, 32, 128), f32),
            pltpu.VMEM((2, 6, 48, 128), f32),
            pltpu.VMEM((2, 6, 48, 128), f32),
            pltpu.VMEM((6, 32, 128), f32),
            pltpu.VMEM((9, 32, 128), f32),
            pltpu.VMEM((2, 9, 32, 128), f32),
            pltpu.VMEM((15, 8, 128), f32),
            pltpu.VMEM((15, 8, 128), f32),
            pltpu.VMEM((2, 6, 8, 128), f32),
            pltpu.VMEM((2, 4, 48, 128), f32),
            pltpu.VMEM((2, 4, 48, 128), f32),
            pltpu.VMEM((2, 6, 32, 128), f32),
            pltpu.VMEM((2, 6, 32, 128), f32),
            pltpu.VMEM((2, 6, 32, 128), f32),
            pltpu.VMEM((2, 6, 32, 128), f32),
            pltpu.SemaphoreType.DMA((8,)),
        ],
        compiler_params=pltpu.CompilerParams(vmem_limit_bytes=32 * 1024 * 1024),
        name="heun_steps",
    )


def body(magnetic, velocity_stack, wavenumber, velocity_owner):
    groups, tiles = lax.axis_size("mode"), lax.axis_size("tile")
    me, tile = lax.axis_index("mode"), lax.axis_index("tile")
    modes = groups * GROUP
    away = jnp.bitwise_xor(me, velocity_owner[0])

    def to_pair(x, first):
        pairs = []
        for i in range(first, groups, 2):
            pairs += [(i, (i + 1) % groups), ((i + 1) % groups, i)]
        return lax.ppermute(x, "mode", pairs)

    def across(x, bit):
        return lax.ppermute(x, "mode", [(i, i ^ bit) for i in range(groups)])

    def to_tile(x, first):
        pairs = []
        for i in range(first, tiles - 1, 2):
            pairs += [(i, i + 1), (i + 1, i)]
        return lax.ppermute(x, "tile", pairs)

    bits = []
    while 2 << len(bits) < groups:
        bits.append(2 << len(bits))
    bits.append(1)
    def choose(x, y, bit):
        return jnp.where(jnp.bitwise_and(away, bit) == 0, x, y)

    pair = to_pair(magnetic, 0)
    flow = choose(velocity_stack, across(velocity_stack, bits[0]), bits[0])
    other = to_pair(magnetic, 1)
    edges = small_kernel(pack_kernel, "pack_edges", shape(9, 8, 128), [VMEM] * 2, LONG)(magnetic, flow)

    def small_exchanges(flow, edges):
        for bit in bits[1:-2]:
            flow = choose(flow, across(flow, bit), bit)
        flow2 = across(flow, bits[-2])
        near, far = to_tile(edges, 0), to_tile(edges, 1)
        odd = tile % 2 == 1
        left, right = jnp.where(odd, near, far), jnp.where(odd, far, near)
        low = lax.broadcasted_iota(jnp.int32, (9, 8, 128), 2) % 8 < 4
        halo = jnp.where(low[6:], left[6:], right[6:])
        strips = jnp.stack([jnp.where(low[:6], left[:6], edges[:6]), jnp.where(low[:6], edges[:6], right[:6])])
        halo2 = across(halo, bits[-2])
        strips_other = to_pair(strips, 1)
        flow, flow2, halo, halo2, strips_other = lax.optimization_barrier((flow, flow2, halo, halo2, strips_other))
        flow, halo = choose(flow, flow2, bits[-2]), choose(halo, halo2, bits[-2])
        message = jnp.concatenate([halo, strips.reshape(12, 8, 128)])
        return flow, across(flow, bits[-1]), message, across(message, bits[-1]), strips_other

    def none(flow, edges):
        message, strips = jnp.zeros((15, 8, 128), f32), jnp.zeros((2, 6, 8, 128), f32)
        return flow, flow, message, message, strips

    *flows, strips_other = lax.cond(velocity_owner[0] >= 0, small_exchanges, none, flow, edges)
    info = jnp.stack(
        [
            lax.rem(wavenumber[0] + modes // 2 + modes - GROUP, modes),
            tile,
            jnp.bitwise_and(away, bits[-1]),
            jnp.bitwise_and(me, 1),
        ]
    ).astype(jnp.int32)
    return steps_call(functools.partial(steps_kernel, modes, tiles))(info, *flows, strips_other, magnetic, pair, other)


def solution(mesh):
    placed = (P("mode", None, None, "tile"), P("mode", None, None, "tile"), P("mode"), P())
    return jax.shard_map(
        body, mesh=mesh, in_specs=placed, out_specs=P("mode", None, None, "tile"), check_vma=False
    )
```

```python
import functools

import jax
import jax.numpy as jnp
from jax import lax
from jax.experimental import pallas as pl
from jax.experimental.pallas import tpu as pltpu
from jax.sharding import PartitionSpec as P

inner_radius = 32.0
f32 = jnp.float32
GROUP = 4
EDGE = 8
SLOTS = 3 * GROUP


def lane_index(rows=8):
    return lax.broadcasted_iota(jnp.int32, (rows, 128), 1)


def turn(x, shift, axis=1):
    if isinstance(shift, int):
        shift %= x.shape[axis]
        if shift == 0:
            return x
    return pltpu.roll(x, shift, axis)


def pack_kernel(field_ref, flow_ref, edges_ref):
    lane = lane_index()
    for comp in range(6):
        total = jnp.zeros((8, 128), f32)
        for zt in range(4):
            for mode in range(GROUP):
                at = 32 * zt + 8 * mode
                piece = turn(field_ref[mode, comp, 8 * zt : 8 * zt + 8, :], at + 4)
                total = jnp.where((lane >= at) & (lane < at + 8), piece, total)
        edges_ref[comp] = total
    for block in range(3):
        total = jnp.zeros((8, 128), f32)
        for part in range(4):
            row = 4 * block + part
            if row < 9:
                for zt in range(4):
                    at = 32 * part + 8 * zt
                    piece = turn(flow_ref[0, row, 8 * zt : 8 * zt + 8, :], at + 4)
                    total = jnp.where((lane >= at) & (lane < at + 8), piece, total)
        edges_ref[6 + block] = total


def pack_fields_kernel(pair_ref, other_ref, edges_ref):
    lane = lane_index()
    for group, field_ref in enumerate((pair_ref, other_ref)):
        for comp in range(6):
            total = jnp.zeros((8, 128), f32)
            for zt in range(4):
                for mode in range(GROUP):
                    at = 32 * zt + 8 * mode
                    piece = turn(field_ref[mode, comp, 8 * zt : 8 * zt + 8, :], at + 4)
                    total = jnp.where((lane >= at) & (lane < at + 8), piece, total)
            edges_ref[group, comp] = total


def emf_of(flow, centre, total, gap):
    steady = flow[0:3]
    swirl_re = (flow[3], flow[5], flow[7])
    swirl_im = (flow[4], flow[6], flow[8])
    out = []
    for comp in range(3):
        i, j = (comp + 1) % 3, (comp + 2) % 3
        real = (
            (steady[i] * centre[2 * j] - steady[j] * centre[2 * i])
            + (swirl_re[i] * total[2 * j] - swirl_re[j] * total[2 * i])
            - (swirl_im[i] * gap[2 * j + 1] - swirl_im[j] * gap[2 * i + 1])
        )
        imag = (
            (steady[i] * centre[2 * j + 1] - steady[j] * centre[2 * i + 1])
            + (swirl_re[i] * total[2 * j + 1] - swirl_re[j] * total[2 * i + 1])
            + (swirl_im[i] * gap[2 * j] - swirl_im[j] * gap[2 * i])
        )
        out += [real, imag]
    return out


def coefficients(radius):
    inner, outer = radius - 1.0, radius + 1.0
    return dict(
        up=1.0 + 0.5 / inner, down=1.0 - 0.5 / outer, flux_up=radius / inner, flux_down=radius / outer,
        inv=1.0 / radius, inv2=1.0 / (radius * radius),
    )


def with_waves(coef, waves):
    return dict(
        coef, waves=waves, decay=6.0 - (waves * waves + 1.0) * coef["inv2"], axial=6.0 - (waves * waves) * coef["inv2"],
        coupling=(2.0 * waves) * coef["inv2"], over=(2.0 * waves) * coef["inv"],
    )


def stencil(field, emf, coef):
    up, down, decay, axial, coupling, over = (coef[n] for n in ("up", "down", "decay", "axial", "coupling", "over"))
    right = [field[i] * up for i in range(6)]
    left = [field[i] * down for i in range(6)]
    place = [field[i] * (decay if i < 4 else axial) for i in range(6)]
    for part in range(2):
        right[2 + part] = right[2 + part] - emf[4 + part]
        left[2 + part] = left[2 + part] + emf[4 + part]
        right[4 + part] = right[4 + part] + emf[2 + part] * coef["flux_up"]
        left[4 + part] = left[4 + part] - emf[2 + part] * coef["flux_down"]
    place[0] = place[0] + (coupling * field[3] - over * emf[5])
    place[1] = place[1] - (coupling * field[2] - over * emf[4])
    place[2] = place[2] - coupling * field[1]
    place[3] = place[3] + coupling * field[0]
    place[4] = place[4] + over * emf[1]
    place[5] = place[5] - over * emf[0]
    return right, left, place


PAD = 8


def tile_rows(zt, shift=0):
    return pl.ds(PAD + 8 * zt + shift, 8)


def add_rows(total, i, get_field, get_emf):
    total = total + (get_field(i, 1) + get_field(i, -1))
    if i < 2:
        total = total - (get_emf(2 + i, 1) - get_emf(2 + i, -1))
    elif i < 4:
        total = total + (get_emf(i - 2, 1) - get_emf(i - 2, -1))
    return total


def wave_at(base, slot, modes):
    return (lax.rem(base + slot, modes) - modes // 2).astype(f32)


def column_radius(column):
    return inner_radius + 0.5 + column.astype(f32)


def steps_kernel(
    modes, tiles, info_ref, flow_ref, flow2_ref, strips_ref, edges_ref, near_ref, far_ref, own_hbm, pair_hbm, other_hbm, out_hbm,
    state, trial, out, strip, strip_trial, inject, flow, flow_strip, emfs, emfs_strip, sums, gaps, rights, lefts, sems,
):
    base, tile, take, odd = info_ref[0], info_ref[1], info_ref[2], info_ref[3]

    places = (GROUP, 2 * GROUP * (1 - odd), 2 * GROUP * odd)
    rows = pl.ds(PAD, 32)
    field_loads = [
        pltpu.make_async_copy(src, state.at[pl.ds(place, GROUP), :, rows], sems.at[4 + i])
        for i, (src, place) in enumerate(zip((own_hbm, pair_hbm, other_hbm), places))
    ]
    for load in field_loads:
        load.start()

    lane8 = lane_index()
    column8 = lane8 % 8
    zeros = jnp.zeros((8, 128), f32)
    for array in (state, trial):

        def clear(k, carry, array=array):
            for i in range(6):
                array[k, i, 0:PAD, :] = zeros
                array[k, i, PAD + 32 : PAD + 40, :] = zeros
            return carry

        lax.fori_loop(0, SLOTS, clear, 0)
    for array in (strip, strip_trial, emfs_strip, emfs):
        for side in range(2):
            for i in range(array.shape[1]):
                array[side, i, 0:PAD, :] = zeros
                array[side, i, PAD + 32 : PAD + 40, :] = zeros

    first_column = tile * 128
    main_coef = coefficients(column_radius(first_column + lane8))
    strip_coef, strip_inside = [], []
    for side in range(2):
        column = first_column + column8 + (124 if side else -4)
        strip_coef.append(with_waves(coefficients(column_radius(column)), wave_at(base, lane8 // 8, modes)))
        strip_inside.append((column >= 0) & (column < tiles * 128))

    tile_odd = lax.rem(tile, 2) == 1
    for comp in range(6):
        sides = []
        for group in range(2):
            edges, near, far = edges_ref[group, comp], near_ref[group, comp], far_ref[group, comp]
            left = jnp.where(tile == 0, 0.0, jnp.where(tile_odd, near, far))
            right = jnp.where(tile == tiles - 1, 0.0, jnp.where(tile_odd, far, near))
            sides.append((jnp.where(column8 < 4, left, edges), jnp.where(column8 < 4, edges, right)))
        for side in range(2):
            own, pair, other = strips_ref[side, comp], sides[0][side], sides[1][side]
            low, high = jnp.where(odd == 1, pair, other), jnp.where(odd == 1, other, pair)
            for zt in range(4):
                value = jnp.where(lane8 < 32, turn(low, -32 * zt), turn(own, 32 - 32 * zt))
                value = jnp.where(lane8 < 64, value, turn(high, 64 - 32 * zt))
                strip[side, comp, tile_rows(zt), :] = jnp.where(lane8 < 96, value, 0.0)

    near = jnp.where(column8 < 4, 124 + column8, column8 - 4)
    for source, wanted in ((flow_ref, 0), (flow2_ref, 1)):

        @pl.when(jnp.where(take == 0, 0, 1) == wanted)
        def _(source=source):
            for r in range(9):
                for zt in range(4):
                    at = slice(8 * zt, 8 * zt + 8)
                    flow[r, at] = source[4 * r + zt]
                    inside = jnp.take_along_axis(source[4 * r + zt], near, axis=1)
                    outside = jnp.take_along_axis(source[36 + r // 4], 32 * (r % 4) + 8 * zt + column8, axis=1)
                    flow_strip[0, r, at] = jnp.where(column8 < 4, outside, inside)
                    flow_strip[1, r, at] = jnp.where(column8 < 4, inside, outside)

    def strips_eval(source, store):
        places = [(side, zt) for side in range(2) for zt in range(4)]
        for side, zt in places:
            at = slice(8 * zt, 8 * zt + 8)
            for i in range(6):
                x = source[side, i, tile_rows(zt), :]
                lower, upper = turn(x, EDGE), turn(x, -EDGE)
                sums[side, i, at], gaps[side, i, at] = lower + upper, lower - upper
        terms = {}
        for side, zt in places:
            at = slice(8 * zt, 8 * zt + 8)
            centre = [source[side, i, tile_rows(zt), :] for i in range(6)]
            velocity = [flow_strip[side, r, at, :] for r in range(9)]
            emf = emf_of(velocity, centre, [sums[side, i, at] for i in range(6)], [gaps[side, i, at] for i in range(6)])
            right, left, terms[side, zt] = stencil(centre, emf, strip_coef[side])
            for i in range(4):
                emfs_strip[side, i, tile_rows(zt), :] = emf[i]
            for i in range(6):
                rights[side, i, at], lefts[side, i, at] = right[i], left[i]
        for side, zt in places:
            at = slice(8 * zt, 8 * zt + 8)
            for i in range(6):
                if store is not None or side:
                    next_column = turn(rights[side, i, at], -1)
                if store is not None or not side:
                    last_column = turn(lefts[side, i, at], 1)
                inject[i, at] = jnp.where(column8 == 3, next_column, inject[i, at]) if side else last_column
                if store is not None:
                    total = add_rows(
                        (next_column + last_column) + terms[side, zt][i], i,
                        lambda c, d: source[side, c, tile_rows(zt, d), :],
                        lambda c, d: emfs_strip[side, c, tile_rows(zt, d), :],
                    )
                    store(side, i, zt, jnp.where(strip_inside[side], total, 0.0))

    def main_eval(source, start, stop, store, after=None):
        def one(k, buffer):
            coef = with_waves(main_coef, wave_at(base, k, modes))
            totals = []
            for zt in range(4):
                centre = [source[k, i, tile_rows(zt), :] for i in range(6)]
                lower = [source[k - 1, i, tile_rows(zt), :] for i in range(6)]
                upper = [source[k + 1, i, tile_rows(zt), :] for i in range(6)]
                total = [lower[i] + upper[i] for i in range(6)]
                gap = [lower[i] - upper[i] for i in range(6)]
                emf = emf_of([flow[r, 8 * zt : 8 * zt + 8, :] for r in range(9)], centre, total, gap)
                for i in range(4):
                    emfs[buffer, i, tile_rows(zt), :] = emf[i]
                right, left, place = stencil(centre, emf, coef)
                total = []
                for i in range(6):
                    edge = pltpu.roll(inject[i, 8 * zt : 8 * zt + 8, :], 124 - EDGE * k, 1)
                    next_column = jnp.where(lane8 == 127, edge, turn(right[i], -1))
                    last_column = jnp.where(lane8 == 0, edge, turn(left[i], 1))
                    total.append((next_column + last_column) + place[i])
                totals.append(total)
            for zt in range(4):
                for i in range(6):
                    total = add_rows(
                        totals[zt][i], i,
                        lambda c, d: source[k, c, tile_rows(zt, d), :],
                        lambda c, d: emfs[buffer, c, tile_rows(zt, d), :],
                    )
                    store(k, i, zt, total)

        def two(n, carry):
            one(start + 2 * n, 0)
            one(start + 2 * n + 1, 1)
            if after is not None:
                after(n)
            return carry

        lax.fori_loop(0, (stop - start) // 2, two, 0)

    def first_main(k, i, zt, total):
        trial[k, i, tile_rows(zt), :] = total

    def second_main(k, i, zt, total):
        state[k, i, tile_rows(zt), :] = 0.5 * state[k, i, tile_rows(zt), :] + 0.005 * total

    def last_main(k, i, zt, total):
        out[k - GROUP, i, 8 * zt : 8 * zt + 8, :] = 0.5 * state[k, i, tile_rows(zt), :] + 0.005 * total

    def first_strip(side, i, zt, total):
        strip_trial[side, i, tile_rows(zt), :] = total

    def second_strip(side, i, zt, total):
        strip[side, i, tile_rows(zt), :] = 0.5 * strip[side, i, tile_rows(zt), :] + 0.005 * total

    strips_eval(strip, first_strip)
    for load in field_loads:
        load.wait()
    main_eval(state, 1, 11, first_main)
    strips_eval(strip_trial, second_strip)
    main_eval(trial, 2, 10, second_main)
    strips_eval(strip, first_strip)
    main_eval(state, 3, 9, first_main)
    strips_eval(strip_trial, None)
    def writing(n):
        done = pl.ds(2 * n, 2)
        return pltpu.make_async_copy(out.at[done], out_hbm.at[done], sems.at[n])

    main_eval(trial, 4, 8, last_main, lambda n: writing(n).start())
    for n in range(GROUP // 2):
        writing(n).wait()


VMEM = pl.BlockSpec(memory_space=pltpu.VMEM)
SMEM = pl.BlockSpec(memory_space=pltpu.SMEM)
ANY = pl.BlockSpec(memory_space=pl.ANY)


SMALL = pl.CostEstimate(flops=8, bytes_accessed=8, transcendentals=0)
LONG = pl.CostEstimate(flops=1_000_000_000, bytes_accessed=100_000_000, transcendentals=0)


def shape(*dims):
    return jax.ShapeDtypeStruct(dims, f32)


def small_kernel(kernel, name, out, in_specs, cost=SMALL):
    out_specs = (VMEM,) * len(out) if isinstance(out, tuple) else VMEM
    return pl.pallas_call(kernel, out_shape=out, in_specs=in_specs, out_specs=out_specs, cost_estimate=cost, name=name)


def steps_call(kernel):
    return pl.pallas_call(
        kernel,
        out_shape=shape(GROUP, 6, 32, 128),
        in_specs=[SMEM] + [VMEM] * 6 + [ANY] * 3,
        out_specs=ANY,
        scratch_shapes=[
            pltpu.VMEM((SLOTS, 6, 48, 128), f32),
            pltpu.VMEM((SLOTS, 6, 48, 128), f32),
            pltpu.VMEM((GROUP, 6, 32, 128), f32),
            pltpu.VMEM((2, 6, 48, 128), f32),
            pltpu.VMEM((2, 6, 48, 128), f32),
            pltpu.VMEM((6, 32, 128), f32),
            pltpu.VMEM((9, 32, 128), f32),
            pltpu.VMEM((2, 9, 32, 128), f32),
            pltpu.VMEM((2, 4, 48, 128), f32),
            pltpu.VMEM((2, 4, 48, 128), f32),
            pltpu.VMEM((2, 6, 32, 128), f32),
            pltpu.VMEM((2, 6, 32, 128), f32),
            pltpu.VMEM((2, 6, 32, 128), f32),
            pltpu.VMEM((2, 6, 32, 128), f32),
            pltpu.SemaphoreType.DMA((8,)),
        ],
        compiler_params=pltpu.CompilerParams(vmem_limit_bytes=32 * 1024 * 1024),
        name="heun_steps",
    )


def body(magnetic, velocity_stack, wavenumber, velocity_owner):
    groups, tiles = lax.axis_size("mode"), lax.axis_size("tile")
    me, tile = lax.axis_index("mode"), lax.axis_index("tile")
    modes = groups * GROUP
    away = jnp.bitwise_xor(me, velocity_owner[0])

    def to_pair(x, first):
        pairs = []
        for i in range(first, groups, 2):
            pairs += [(i, (i + 1) % groups), ((i + 1) % groups, i)]
        return lax.ppermute(x, "mode", pairs)

    def across(x, bit):
        return lax.ppermute(x, "mode", [(i, i ^ bit) for i in range(groups)])

    def to_tile(x, first):
        pairs = []
        for i in range(first, tiles, 2):
            pairs += [(i, (i + 1) % tiles), ((i + 1) % tiles, i)]
        return lax.ppermute(x, "tile", pairs)

    bits = []
    while 2 << len(bits) < groups:
        bits.append(2 << len(bits))
    bits.append(1)
    def choose(x, y, bit):
        return jnp.where(jnp.bitwise_and(away, bit) == 0, x, y)

    pair = to_pair(magnetic, 0)
    flow = choose(velocity_stack, across(velocity_stack, bits[0]), bits[0])
    other = to_pair(magnetic, 1)
    info = jnp.stack(
        [
            lax.rem(wavenumber[0] + modes // 2 + modes - GROUP, modes),
            tile,
            jnp.bitwise_and(away, bits[-1]),
            jnp.bitwise_and(me, 1),
        ]
    ).astype(jnp.int32)
    flow, info = lax.optimization_barrier((flow, info))
    edges = small_kernel(pack_kernel, "pack_edges", shape(9, 8, 128), [VMEM] * 2, LONG)(magnetic, flow)

    def beyond(edges):
        near, far = to_tile(edges, 0), to_tile(edges, 1)
        odd = tile % 2 == 1
        left = jnp.where(tile == 0, 0.0, jnp.where(odd, near, far))
        right = jnp.where(tile == tiles - 1, 0.0, jnp.where(odd, far, near))
        return left, right, lax.broadcasted_iota(jnp.int32, edges.shape, edges.ndim - 1) % 8 < 4

    def as_strips(edges, left, right, low):
        return jnp.stack([jnp.where(low, left, edges), jnp.where(low, edges, right)])

    def middle_rounds(flow, edges):
        for bit in bits[1:-2]:
            flow = choose(flow, across(flow, bit), bit)
        flow2 = across(flow, bits[-2])
        left, right, low = beyond(edges)
        strips = as_strips(edges[:6], left[:6], right[:6], low[:6])
        halo = jnp.where(low[6:], left[6:], right[6:])
        for bit in bits[1:-2]:
            halo = choose(halo, across(halo, bit), bit)
        halo2 = across(halo, bits[-2])
        flow, flow2, halo, halo2 = lax.optimization_barrier((flow, flow2, halo, halo2))
        flow, halo = choose(flow, flow2, bits[-2]), choose(halo, halo2, bits[-2])
        return jnp.concatenate([flow.reshape(36, 8, 128), halo]), strips

    def no_rounds(flow, edges):
        return jnp.zeros((39, 8, 128), f32), jnp.zeros((2, 6, 8, 128), f32)

    def neighbours(pair, other):
        edges = small_kernel(pack_fields_kernel, "pack_field_edges", shape(2, 6, 8, 128), [VMEM] * 2)(pair, other)
        near, far = to_tile(edges, 0), to_tile(edges, 1)
        return edges, near, far

    def no_neighbours(pair, other):
        edges = jnp.zeros((2, 6, 8, 128), f32)
        return edges, edges, edges

    flow, strips = lax.cond(velocity_owner[0] >= 0, middle_rounds, no_rounds, flow, edges)
    flow2 = across(flow, 1)
    edges, near, far = lax.cond(velocity_owner[0] < groups, neighbours, no_neighbours, pair, other)
    return steps_call(functools.partial(steps_kernel, modes, tiles))(info, flow, flow2, strips, edges, near, far, magnetic, pair, other)


def solution(mesh):
    placed = (P("mode", None, None, "tile"), P("mode", None, None, "tile"), P("mode"), P())
    return jax.shard_map(
        body, mesh=mesh, in_specs=placed, out_specs=P("mode", None, None, "tile"), check_vma=False
    )
```

```python
import functools

import jax
import jax.numpy as jnp
from jax import lax
from jax.experimental import pallas as pl
from jax.experimental.pallas import tpu as pltpu
from jax.sharding import PartitionSpec as P

inner_radius = 32.0
f32 = jnp.float32
GROUP = 4
EDGE = 8
SLOTS = 3 * GROUP


def lane_index(rows=8):
    return lax.broadcasted_iota(jnp.int32, (rows, 128), 1)


def turn(x, shift, axis=1):
    if isinstance(shift, int):
        shift %= x.shape[axis]
        if shift == 0:
            return x
    return pltpu.roll(x, shift, axis)


def pack_kernel(field_ref, flow_ref, edges_ref):
    lane = lane_index()
    for comp in range(6):
        total = jnp.zeros((8, 128), f32)
        for zt in range(4):
            for mode in range(GROUP):
                at = 32 * zt + 8 * mode
                piece = turn(field_ref[mode, comp, 8 * zt : 8 * zt + 8, :], at + 4)
                total = jnp.where((lane >= at) & (lane < at + 8), piece, total)
        edges_ref[comp] = total
    for block in range(3):
        total = jnp.zeros((8, 128), f32)
        for part in range(4):
            row = 4 * block + part
            if row < 9:
                for zt in range(4):
                    at = 32 * part + 8 * zt
                    piece = turn(flow_ref[0, row, 8 * zt : 8 * zt + 8, :], at + 4)
                    total = jnp.where((lane >= at) & (lane < at + 8), piece, total)
        edges_ref[6 + block] = total


def pack_fields_kernel(pair_ref, other_ref, edges_ref):
    lane = lane_index()
    for group, field_ref in enumerate((pair_ref, other_ref)):
        for comp in range(6):
            total = jnp.zeros((8, 128), f32)
            for zt in range(4):
                for mode in range(GROUP):
                    at = 32 * zt + 8 * mode
                    piece = turn(field_ref[mode, comp, 8 * zt : 8 * zt + 8, :], at + 4)
                    total = jnp.where((lane >= at) & (lane < at + 8), piece, total)
            edges_ref[group, comp] = total


def emf_of(flow, centre, total, gap):
    steady = flow[0:3]
    swirl_re = (flow[3], flow[5], flow[7])
    swirl_im = (flow[4], flow[6], flow[8])
    out = []
    for comp in range(3):
        i, j = (comp + 1) % 3, (comp + 2) % 3
        real = (
            (steady[i] * centre[2 * j] - steady[j] * centre[2 * i])
            + (swirl_re[i] * total[2 * j] - swirl_re[j] * total[2 * i])
            - (swirl_im[i] * gap[2 * j + 1] - swirl_im[j] * gap[2 * i + 1])
        )
        imag = (
            (steady[i] * centre[2 * j + 1] - steady[j] * centre[2 * i + 1])
            + (swirl_re[i] * total[2 * j + 1] - swirl_re[j] * total[2 * i + 1])
            + (swirl_im[i] * gap[2 * j] - swirl_im[j] * gap[2 * i])
        )
        out += [real, imag]
    return out


def coefficients(radius):
    inner, outer = radius - 1.0, radius + 1.0
    return dict(
        up=1.0 + 0.5 / inner, down=1.0 - 0.5 / outer, flux_up=radius / inner, flux_down=radius / outer,
        inv=1.0 / radius, inv2=1.0 / (radius * radius),
    )


def with_waves(coef, waves):
    return dict(
        coef, waves=waves, decay=6.0 - (waves * waves + 1.0) * coef["inv2"], axial=6.0 - (waves * waves) * coef["inv2"],
        coupling=(2.0 * waves) * coef["inv2"], over=(2.0 * waves) * coef["inv"],
    )


def stencil(field, emf, coef):
    up, down, decay, axial, coupling, over = (coef[n] for n in ("up", "down", "decay", "axial", "coupling", "over"))
    right = [field[i] * up for i in range(6)]
    left = [field[i] * down for i in range(6)]
    place = [field[i] * (decay if i < 4 else axial) for i in range(6)]
    for part in range(2):
        right[2 + part] = right[2 + part] - emf[4 + part]
        left[2 + part] = left[2 + part] + emf[4 + part]
        right[4 + part] = right[4 + part] + emf[2 + part] * coef["flux_up"]
        left[4 + part] = left[4 + part] - emf[2 + part] * coef["flux_down"]
    place[0] = place[0] + (coupling * field[3] - over * emf[5])
    place[1] = place[1] - (coupling * field[2] - over * emf[4])
    place[2] = place[2] - coupling * field[1]
    place[3] = place[3] + coupling * field[0]
    place[4] = place[4] + over * emf[1]
    place[5] = place[5] - over * emf[0]
    return right, left, place


PAD = 8


def tile_rows(zt, shift=0):
    return pl.ds(PAD + 8 * zt + shift, 8)


def add_rows(total, i, get_field, get_emf):
    total = total + (get_field(i, 1) + get_field(i, -1))
    if i < 2:
        total = total - (get_emf(2 + i, 1) - get_emf(2 + i, -1))
    elif i < 4:
        total = total + (get_emf(i - 2, 1) - get_emf(i - 2, -1))
    return total


def wave_at(base, slot, modes):
    return (lax.rem(base + slot, modes) - modes // 2).astype(f32)


def column_radius(column):
    return inner_radius + 0.5 + column.astype(f32)


def steps_kernel(
    modes, tiles, info_ref, flow_ref, flow2_ref, strips_ref, edges_ref, near_ref, far_ref, own_hbm, pair_hbm, other_hbm, out_hbm,
    state, trial, out, strip, strip_trial, inject, flow, flow_strip, emfs, emfs_strip, sums, gaps, rights, lefts, sems,
):
    base, tile, take, odd = info_ref[0], info_ref[1], info_ref[2], info_ref[3]

    places = (GROUP, 2 * GROUP * (1 - odd), 2 * GROUP * odd)
    rows = pl.ds(PAD, 32)
    field_loads = [
        pltpu.make_async_copy(src, state.at[pl.ds(place, GROUP), :, rows], sems.at[4 + i])
        for i, (src, place) in enumerate(zip((own_hbm, pair_hbm, other_hbm), places))
    ]
    for load in field_loads:
        load.start()

    lane8 = lane_index()
    column8 = lane8 % 8
    zeros = jnp.zeros((8, 128), f32)
    for array in (state, trial):

        def clear(k, carry, array=array):
            for i in range(6):
                array[k, i, 0:PAD, :] = zeros
                array[k, i, PAD + 32 : PAD + 40, :] = zeros
            return carry

        lax.fori_loop(0, SLOTS, clear, 0)
    for array in (strip, strip_trial, emfs_strip, emfs):
        for side in range(2):
            for i in range(array.shape[1]):
                array[side, i, 0:PAD, :] = zeros
                array[side, i, PAD + 32 : PAD + 40, :] = zeros

    first_column = tile * 128
    main_coef = coefficients(column_radius(first_column + lane8))
    strip_coef, strip_inside = [], []
    for side in range(2):
        column = first_column + column8 + (124 if side else -4)
        strip_coef.append(with_waves(coefficients(column_radius(column)), wave_at(base, lane8 // 8, modes)))
        strip_inside.append((column >= 0) & (column < tiles * 128))

    tile_odd = lax.rem(tile, 2) == 1
    for comp in range(6):
        sides = []
        for group in range(2):
            edges, near, far = edges_ref[group, comp], near_ref[group, comp], far_ref[group, comp]
            left = jnp.where(tile == 0, 0.0, jnp.where(tile_odd, near, far))
            right = jnp.where(tile == tiles - 1, 0.0, jnp.where(tile_odd, far, near))
            sides.append((jnp.where(column8 < 4, left, edges), jnp.where(column8 < 4, edges, right)))
        for side in range(2):
            own, pair, other = strips_ref[side, comp], sides[0][side], sides[1][side]
            low, high = jnp.where(odd == 1, pair, other), jnp.where(odd == 1, other, pair)
            for zt in range(4):
                value = jnp.where(lane8 < 32, turn(low, -32 * zt), turn(own, 32 - 32 * zt))
                value = jnp.where(lane8 < 64, value, turn(high, 64 - 32 * zt))
                strip[side, comp, tile_rows(zt), :] = jnp.where(lane8 < 96, value, 0.0)

    near = jnp.where(column8 < 4, 124 + column8, column8 - 4)
    for source, wanted in ((flow_ref, 0), (flow2_ref, 1)):

        @pl.when(jnp.where(take == 0, 0, 1) == wanted)
        def _(source=source):
            for r in range(9):
                for zt in range(4):
                    at = slice(8 * zt, 8 * zt + 8)
                    flow[r, at] = source[4 * r + zt]
                    inside = jnp.take_along_axis(source[4 * r + zt], near, axis=1)
                    outside = jnp.take_along_axis(source[36 + r // 4], 32 * (r % 4) + 8 * zt + column8, axis=1)
                    flow_strip[0, r, at] = jnp.where(column8 < 4, outside, inside)
                    flow_strip[1, r, at] = jnp.where(column8 < 4, inside, outside)

    def strips_eval(source, store):
        places = [(side, zt) for side in range(2) for zt in range(4)]
        for side, zt in places:
            at = slice(8 * zt, 8 * zt + 8)
            for i in range(6):
                x = source[side, i, tile_rows(zt), :]
                lower, upper = turn(x, EDGE), turn(x, -EDGE)
                sums[side, i, at], gaps[side, i, at] = lower + upper, lower - upper
        terms = {}
        for side, zt in places:
            at = slice(8 * zt, 8 * zt + 8)
            centre = [source[side, i, tile_rows(zt), :] for i in range(6)]
            velocity = [flow_strip[side, r, at, :] for r in range(9)]
            emf = emf_of(velocity, centre, [sums[side, i, at] for i in range(6)], [gaps[side, i, at] for i in range(6)])
            right, left, terms[side, zt] = stencil(centre, emf, strip_coef[side])
            if store is not None:
                for i in range(4):
                    emfs_strip[side, i, tile_rows(zt), :] = emf[i]
            for i in range(6):
                if store is not None or side:
                    rights[side, i, at] = right[i]
                if store is not None or not side:
                    lefts[side, i, at] = left[i]
        for side, zt in places:
            at = slice(8 * zt, 8 * zt + 8)
            for i in range(6):
                if store is not None or side:
                    next_column = turn(rights[side, i, at], -1)
                if store is not None or not side:
                    last_column = turn(lefts[side, i, at], 1)
                inject[i, at] = jnp.where(column8 == 3, next_column, inject[i, at]) if side else last_column
                if store is not None:
                    total = add_rows(
                        (next_column + last_column) + terms[side, zt][i], i,
                        lambda c, d: source[side, c, tile_rows(zt, d), :],
                        lambda c, d: emfs_strip[side, c, tile_rows(zt, d), :],
                    )
                    store(side, i, zt, jnp.where(strip_inside[side], total, 0.0))

    def main_eval(source, start, stop, store, after=None):
        def one(k, buffer):
            coef = with_waves(main_coef, wave_at(base, k, modes))
            totals = []
            for zt in range(4):
                centre = [source[k, i, tile_rows(zt), :] for i in range(6)]
                lower = [source[k - 1, i, tile_rows(zt), :] for i in range(6)]
                upper = [source[k + 1, i, tile_rows(zt), :] for i in range(6)]
                total = [lower[i] + upper[i] for i in range(6)]
                gap = [lower[i] - upper[i] for i in range(6)]
                emf = emf_of([flow[r, 8 * zt : 8 * zt + 8, :] for r in range(9)], centre, total, gap)
                for i in range(4):
                    emfs[buffer, i, tile_rows(zt), :] = emf[i]
                right, left, place = stencil(centre, emf, coef)
                total = []
                for i in range(6):
                    edge = pltpu.roll(inject[i, 8 * zt : 8 * zt + 8, :], 124 - EDGE * k, 1)
                    next_column = jnp.where(lane8 == 127, edge, turn(right[i], -1))
                    last_column = jnp.where(lane8 == 0, edge, turn(left[i], 1))
                    total.append((next_column + last_column) + place[i])
                totals.append(total)
            for zt in range(4):
                for i in range(6):
                    total = add_rows(
                        totals[zt][i], i,
                        lambda c, d: source[k, c, tile_rows(zt, d), :],
                        lambda c, d: emfs[buffer, c, tile_rows(zt, d), :],
                    )
                    store(k, i, zt, total)

        def two(n, carry):
            one(start + 2 * n, 0)
            one(start + 2 * n + 1, 1)
            if after is not None:
                after(n)
            return carry

        for n in range((stop - start) // 2):
            two(n, 0)

    def first_main(k, i, zt, total):
        trial[k, i, tile_rows(zt), :] = total

    def second_main(k, i, zt, total):
        state[k, i, tile_rows(zt), :] = 0.5 * state[k, i, tile_rows(zt), :] + 0.005 * total

    def last_main(k, i, zt, total):
        out[k - GROUP, i, 8 * zt : 8 * zt + 8, :] = 0.5 * state[k, i, tile_rows(zt), :] + 0.005 * total

    def first_strip(side, i, zt, total):
        strip_trial[side, i, tile_rows(zt), :] = total

    def second_strip(side, i, zt, total):
        strip[side, i, tile_rows(zt), :] = 0.5 * strip[side, i, tile_rows(zt), :] + 0.005 * total

    strips_eval(strip, first_strip)
    for load in field_loads:
        load.wait()
    main_eval(state, 1, 11, first_main)
    strips_eval(strip_trial, second_strip)
    main_eval(trial, 2, 10, second_main)
    strips_eval(strip, first_strip)
    main_eval(state, 3, 9, first_main)
    strips_eval(strip_trial, None)
    def writing(n):
        done = pl.ds(2 * n, 2)
        return pltpu.make_async_copy(out.at[done], out_hbm.at[done], sems.at[n])

    main_eval(trial, 4, 8, last_main, lambda n: writing(n).start())
    for n in range(GROUP // 2):
        writing(n).wait()


VMEM = pl.BlockSpec(memory_space=pltpu.VMEM)
SMEM = pl.BlockSpec(memory_space=pltpu.SMEM)
ANY = pl.BlockSpec(memory_space=pl.ANY)


SMALL = pl.CostEstimate(flops=8, bytes_accessed=8, transcendentals=0)
LONG = pl.CostEstimate(flops=1_000_000_000, bytes_accessed=100_000_000, transcendentals=0)


def shape(*dims):
    return jax.ShapeDtypeStruct(dims, f32)


def small_kernel(kernel, name, out, in_specs, cost=SMALL):
    out_specs = (VMEM,) * len(out) if isinstance(out, tuple) else VMEM
    return pl.pallas_call(kernel, out_shape=out, in_specs=in_specs, out_specs=out_specs, cost_estimate=cost, name=name)


def steps_call(kernel):
    return pl.pallas_call(
        kernel,
        out_shape=shape(GROUP, 6, 32, 128),
        in_specs=[SMEM] + [VMEM] * 6 + [ANY] * 3,
        out_specs=ANY,
        scratch_shapes=[
            pltpu.VMEM((SLOTS, 6, 48, 128), f32),
            pltpu.VMEM((SLOTS, 6, 48, 128), f32),
            pltpu.VMEM((GROUP, 6, 32, 128), f32),
            pltpu.VMEM((2, 6, 48, 128), f32),
            pltpu.VMEM((2, 6, 48, 128), f32),
            pltpu.VMEM((6, 32, 128), f32),
            pltpu.VMEM((9, 32, 128), f32),
            pltpu.VMEM((2, 9, 32, 128), f32),
            pltpu.VMEM((2, 4, 48, 128), f32),
            pltpu.VMEM((2, 4, 48, 128), f32),
            pltpu.VMEM((2, 6, 32, 128), f32),
            pltpu.VMEM((2, 6, 32, 128), f32),
            pltpu.VMEM((2, 6, 32, 128), f32),
            pltpu.VMEM((2, 6, 32, 128), f32),
            pltpu.SemaphoreType.DMA((8,)),
        ],
        compiler_params=pltpu.CompilerParams(vmem_limit_bytes=32 * 1024 * 1024),
        name="heun_steps",
    )


def body(magnetic, velocity_stack, wavenumber, velocity_owner):
    groups, tiles = lax.axis_size("mode"), lax.axis_size("tile")
    me, tile = lax.axis_index("mode"), lax.axis_index("tile")
    modes = groups * GROUP
    away = jnp.bitwise_xor(me, velocity_owner[0])

    def to_pair(x, first):
        pairs = []
        for i in range(first, groups, 2):
            pairs += [(i, (i + 1) % groups), ((i + 1) % groups, i)]
        return lax.ppermute(x, "mode", pairs)

    def across(x, bit):
        return lax.ppermute(x, "mode", [(i, i ^ bit) for i in range(groups)])

    def to_tile(x, first):
        pairs = []
        for i in range(first, tiles, 2):
            pairs += [(i, (i + 1) % tiles), ((i + 1) % tiles, i)]
        return lax.ppermute(x, "tile", pairs)

    bits = []
    while 2 << len(bits) < groups:
        bits.append(2 << len(bits))
    bits.append(1)
    def choose(x, y, bit):
        return jnp.where(jnp.bitwise_and(away, bit) == 0, x, y)

    pair = to_pair(magnetic, 0)
    flow = choose(velocity_stack, across(velocity_stack, bits[0]), bits[0])
    other = to_pair(magnetic, 1)
    info = jnp.stack(
        [
            lax.rem(wavenumber[0] + modes // 2 + modes - GROUP, modes),
            tile,
            jnp.bitwise_and(away, bits[-1]),
            jnp.bitwise_and(me, 1),
        ]
    ).astype(jnp.int32)
    flow, info = lax.optimization_barrier((flow, info))
    edges = small_kernel(pack_kernel, "pack_edges", shape(9, 8, 128), [VMEM] * 2, LONG)(magnetic, flow)

    def beyond(edges):
        near, far = to_tile(edges, 0), to_tile(edges, 1)
        odd = tile % 2 == 1
        left = jnp.where(tile == 0, 0.0, jnp.where(odd, near, far))
        right = jnp.where(tile == tiles - 1, 0.0, jnp.where(odd, far, near))
        return left, right, lax.broadcasted_iota(jnp.int32, edges.shape, edges.ndim - 1) % 8 < 4

    def as_strips(edges, left, right, low):
        return jnp.stack([jnp.where(low, left, edges), jnp.where(low, edges, right)])

    def middle_rounds(flow, edges):
        for bit in bits[1:-2]:
            flow = choose(flow, across(flow, bit), bit)
        flow2 = across(flow, bits[-2])
        left, right, low = beyond(edges)
        strips = as_strips(edges[:6], left[:6], right[:6], low[:6])
        halo = jnp.where(low[6:], left[6:], right[6:])
        for bit in bits[1:-2]:
            halo = choose(halo, across(halo, bit), bit)
        halo2 = across(halo, bits[-2])
        flow, flow2, halo, halo2 = lax.optimization_barrier((flow, flow2, halo, halo2))
        flow, halo = choose(flow, flow2, bits[-2]), choose(halo, halo2, bits[-2])
        return jnp.concatenate([flow.reshape(36, 8, 128), halo]), strips

    def no_rounds(flow, edges):
        return jnp.zeros((39, 8, 128), f32), jnp.zeros((2, 6, 8, 128), f32)

    def neighbours(pair, other):
        edges = small_kernel(pack_fields_kernel, "pack_field_edges", shape(2, 6, 8, 128), [VMEM] * 2)(pair, other)
        near, far = to_tile(edges, 0), to_tile(edges, 1)
        return edges, near, far

    def no_neighbours(pair, other):
        edges = jnp.zeros((2, 6, 8, 128), f32)
        return edges, edges, edges

    flow, strips = lax.cond(velocity_owner[0] >= 0, middle_rounds, no_rounds, flow, edges)
    flow2 = across(flow, 1)
    edges, near, far = lax.cond(velocity_owner[0] < groups, neighbours, no_neighbours, pair, other)
    return steps_call(functools.partial(steps_kernel, modes, tiles))(info, flow, flow2, strips, edges, near, far, magnetic, pair, other)


def solution(mesh):
    placed = (P("mode", None, None, "tile"), P("mode", None, None, "tile"), P("mode"), P())
    return jax.shard_map(
        body, mesh=mesh, in_specs=placed, out_specs=P("mode", None, None, "tile"), check_vma=False
    )
```

```python
import functools

import jax
import jax.numpy as jnp
from jax import lax
from jax.experimental import pallas as pl
from jax.experimental.pallas import tpu as pltpu
from jax.sharding import PartitionSpec as P

inner_radius = 32.0
f32 = jnp.float32
GROUP = 4
EDGE = 8
SLOTS = 3 * GROUP


def lane_index(rows=8):
    return lax.broadcasted_iota(jnp.int32, (rows, 128), 1)


def turn(x, shift, axis=1):
    if isinstance(shift, int):
        shift %= x.shape[axis]
        if shift == 0:
            return x
    return pltpu.roll(x, shift, axis)


def pack_kernel(field_ref, flow_ref, edges_ref):
    lane = lane_index()
    for comp in range(6):
        total = jnp.zeros((8, 128), f32)
        for zt in range(4):
            for mode in range(GROUP):
                at = 32 * zt + 8 * mode
                piece = turn(field_ref[mode, comp, 8 * zt : 8 * zt + 8, :], at + 4)
                total = jnp.where((lane >= at) & (lane < at + 8), piece, total)
        edges_ref[comp] = total
    for block in range(3):
        total = jnp.zeros((8, 128), f32)
        for part in range(4):
            row = 4 * block + part
            if row < 9:
                for zt in range(4):
                    at = 32 * part + 8 * zt
                    piece = turn(flow_ref[0, row, 8 * zt : 8 * zt + 8, :], at + 4)
                    total = jnp.where((lane >= at) & (lane < at + 8), piece, total)
        edges_ref[6 + block] = total


def pack_fields_kernel(pair_ref, other_ref, edges_ref):
    lane = lane_index()
    for group, field_ref in enumerate((pair_ref, other_ref)):
        for comp in range(6):
            total = jnp.zeros((8, 128), f32)
            for zt in range(4):
                for mode in range(GROUP):
                    at = 32 * zt + 8 * mode
                    piece = turn(field_ref[mode, comp, 8 * zt : 8 * zt + 8, :], at + 4)
                    total = jnp.where((lane >= at) & (lane < at + 8), piece, total)
            edges_ref[group, comp] = total


def emf_of(flow, centre, total, gap):
    steady = flow[0:3]
    swirl_re = (flow[3], flow[5], flow[7])
    swirl_im = (flow[4], flow[6], flow[8])
    out = []
    for comp in range(3):
        i, j = (comp + 1) % 3, (comp + 2) % 3
        real = (
            (steady[i] * centre[2 * j] - steady[j] * centre[2 * i])
            + (swirl_re[i] * total[2 * j] - swirl_re[j] * total[2 * i])
            - (swirl_im[i] * gap[2 * j + 1] - swirl_im[j] * gap[2 * i + 1])
        )
        imag = (
            (steady[i] * centre[2 * j + 1] - steady[j] * centre[2 * i + 1])
            + (swirl_re[i] * total[2 * j + 1] - swirl_re[j] * total[2 * i + 1])
            + (swirl_im[i] * gap[2 * j] - swirl_im[j] * gap[2 * i])
        )
        out += [real, imag]
    return out


def coefficients(radius):
    inner, outer = radius - 1.0, radius + 1.0
    return dict(
        up=1.0 + 0.5 / inner, down=1.0 - 0.5 / outer, flux_up=radius / inner, flux_down=radius / outer,
        inv=1.0 / radius, inv2=1.0 / (radius * radius),
    )


def with_waves(coef, waves):
    return dict(
        coef, waves=waves, decay=6.0 - (waves * waves + 1.0) * coef["inv2"], axial=6.0 - (waves * waves) * coef["inv2"],
        coupling=(2.0 * waves) * coef["inv2"], over=(2.0 * waves) * coef["inv"],
    )


def stencil(field, emf, coef):
    up, down, decay, axial, coupling, over = (coef[n] for n in ("up", "down", "decay", "axial", "coupling", "over"))
    right = [field[i] * up for i in range(6)]
    left = [field[i] * down for i in range(6)]
    place = [field[i] * (decay if i < 4 else axial) for i in range(6)]
    for part in range(2):
        right[2 + part] = right[2 + part] - emf[4 + part]
        left[2 + part] = left[2 + part] + emf[4 + part]
        right[4 + part] = right[4 + part] + emf[2 + part] * coef["flux_up"]
        left[4 + part] = left[4 + part] - emf[2 + part] * coef["flux_down"]
    place[0] = place[0] + (coupling * field[3] - over * emf[5])
    place[1] = place[1] - (coupling * field[2] - over * emf[4])
    place[2] = place[2] - coupling * field[1]
    place[3] = place[3] + coupling * field[0]
    place[4] = place[4] + over * emf[1]
    place[5] = place[5] - over * emf[0]
    return right, left, place


PAD = 8


def tile_rows(zt, shift=0):
    return pl.ds(PAD + 8 * zt + shift, 8)


def add_rows(total, i, get_field, get_emf):
    total = total + (get_field(i, 1) + get_field(i, -1))
    if i < 2:
        total = total - (get_emf(2 + i, 1) - get_emf(2 + i, -1))
    elif i < 4:
        total = total + (get_emf(i - 2, 1) - get_emf(i - 2, -1))
    return total


def wave_at(base, slot, modes):
    return (lax.rem(base + slot, modes) - modes // 2).astype(f32)


def column_radius(column):
    return inner_radius + 0.5 + column.astype(f32)


def steps_kernel(
    modes, tiles, info_ref, flow_ref, flow2_ref, strips_ref, edges_ref, near_ref, far_ref, own_hbm, pair_hbm, other_hbm, out_hbm,
    state, trial, out, strip, strip_trial, inject, flow, flow_strip, emfs, emfs_strip, sums, gaps, rights, lefts, sems,
):
    base, tile, take, odd = info_ref[0], info_ref[1], info_ref[2], info_ref[3]

    places = (GROUP, 2 * GROUP * (1 - odd), 2 * GROUP * odd)
    rows = pl.ds(PAD, 32)
    field_loads = [
        pltpu.make_async_copy(src, state.at[pl.ds(place, GROUP), :, rows], sems.at[4 + i])
        for i, (src, place) in enumerate(zip((own_hbm, pair_hbm, other_hbm), places))
    ]
    for load in field_loads:
        load.start()

    lane8 = lane_index()
    column8 = lane8 % 8
    zeros = jnp.zeros((8, 128), f32)
    for array, slots in ((state, range(1, 11)), (trial, range(2, 10))):
        for k in slots:
            for i in range(6):
                array[k, i, 0:PAD, :] = zeros
                array[k, i, PAD + 32 : PAD + 40, :] = zeros
    for array in (strip, strip_trial, emfs_strip, emfs):
        for side in range(2):
            for i in range(array.shape[1]):
                array[side, i, 0:PAD, :] = zeros
                array[side, i, PAD + 32 : PAD + 40, :] = zeros

    first_column = tile * 128
    main_coef = coefficients(column_radius(first_column + lane8))
    strip_coef, strip_inside = [], []
    for side in range(2):
        column = first_column + column8 + (124 if side else -4)
        strip_coef.append(with_waves(coefficients(column_radius(column)), wave_at(base, lane8 // 8, modes)))
        strip_inside.append((column >= 0) & (column < tiles * 128))

    tile_odd = lax.rem(tile, 2) == 1
    for comp in range(6):
        sides = []
        for group in range(2):
            edges, near, far = edges_ref[group, comp], near_ref[group, comp], far_ref[group, comp]
            left = jnp.where(tile == 0, 0.0, jnp.where(tile_odd, near, far))
            right = jnp.where(tile == tiles - 1, 0.0, jnp.where(tile_odd, far, near))
            sides.append((jnp.where(column8 < 4, left, edges), jnp.where(column8 < 4, edges, right)))
        for side in range(2):
            own, pair, other = strips_ref[side, comp], sides[0][side], sides[1][side]
            low, high = jnp.where(odd == 1, pair, other), jnp.where(odd == 1, other, pair)
            for zt in range(4):
                value = jnp.where(lane8 < 32, turn(low, -32 * zt), turn(own, 32 - 32 * zt))
                value = jnp.where(lane8 < 64, value, turn(high, 64 - 32 * zt))
                strip[side, comp, tile_rows(zt), :] = jnp.where(lane8 < 96, value, 0.0)

    near = jnp.where(column8 < 4, 124 + column8, column8 - 4)
    halos = [jnp.where(take == 0, flow_ref[36 + block], flow2_ref[36 + block]) for block in range(3)]
    for r in range(9):
        for zt in range(4):
            at = slice(8 * zt, 8 * zt + 8)
            value = jnp.where(take == 0, flow_ref[4 * r + zt], flow2_ref[4 * r + zt])
            flow[r, at] = value
            inside = jnp.take_along_axis(value, near, axis=1)
            outside = jnp.take_along_axis(halos[r // 4], 32 * (r % 4) + 8 * zt + column8, axis=1)
            flow_strip[0, r, at] = jnp.where(column8 < 4, outside, inside)
            flow_strip[1, r, at] = jnp.where(column8 < 4, inside, outside)

    def strips_eval(source, store):
        places = [(side, zt) for side in range(2) for zt in range(4)]
        for side, zt in places:
            at = slice(8 * zt, 8 * zt + 8)
            for i in range(6):
                x = source[side, i, tile_rows(zt), :]
                lower, upper = turn(x, EDGE), turn(x, -EDGE)
                sums[side, i, at], gaps[side, i, at] = lower + upper, lower - upper
        terms = {}
        for side, zt in places:
            at = slice(8 * zt, 8 * zt + 8)
            centre = [source[side, i, tile_rows(zt), :] for i in range(6)]
            velocity = [flow_strip[side, r, at, :] for r in range(9)]
            emf = emf_of(velocity, centre, [sums[side, i, at] for i in range(6)], [gaps[side, i, at] for i in range(6)])
            right, left, terms[side, zt] = stencil(centre, emf, strip_coef[side])
            if store is not None:
                for i in range(4):
                    emfs_strip[side, i, tile_rows(zt), :] = emf[i]
            for i in range(6):
                if store is not None or side:
                    rights[side, i, at] = right[i]
                if store is not None or not side:
                    lefts[side, i, at] = left[i]
        for side, zt in places:
            at = slice(8 * zt, 8 * zt + 8)
            for i in range(6):
                if store is not None or side:
                    next_column = turn(rights[side, i, at], -1)
                if store is not None or not side:
                    last_column = turn(lefts[side, i, at], 1)
                inject[i, at] = jnp.where(column8 == 3, next_column, inject[i, at]) if side else last_column
                if store is not None:
                    total = add_rows(
                        (next_column + last_column) + terms[side, zt][i], i,
                        lambda c, d: source[side, c, tile_rows(zt, d), :],
                        lambda c, d: emfs_strip[side, c, tile_rows(zt, d), :],
                    )
                    store(side, i, zt, jnp.where(strip_inside[side], total, 0.0))

    def main_eval(source, start, stop, store, after=None):
        def one(k, buffer):
            coef = with_waves(main_coef, wave_at(base, k, modes))
            totals = []
            for zt in range(4):
                centre = [source[k, i, tile_rows(zt), :] for i in range(6)]
                lower = [source[k - 1, i, tile_rows(zt), :] for i in range(6)]
                upper = [source[k + 1, i, tile_rows(zt), :] for i in range(6)]
                total = [lower[i] + upper[i] for i in range(6)]
                gap = [lower[i] - upper[i] for i in range(6)]
                emf = emf_of([flow[r, 8 * zt : 8 * zt + 8, :] for r in range(9)], centre, total, gap)
                for i in range(4):
                    emfs[buffer, i, tile_rows(zt), :] = emf[i]
                right, left, place = stencil(centre, emf, coef)
                total = []
                for i in range(6):
                    edge = pltpu.roll(inject[i, 8 * zt : 8 * zt + 8, :], 124 - EDGE * k, 1)
                    next_column = jnp.where(lane8 == 127, edge, turn(right[i], -1))
                    last_column = jnp.where(lane8 == 0, edge, turn(left[i], 1))
                    total.append((next_column + last_column) + place[i])
                totals.append(total)
            for zt in range(4):
                for i in range(6):
                    total = add_rows(
                        totals[zt][i], i,
                        lambda c, d: source[k, c, tile_rows(zt, d), :],
                        lambda c, d: emfs[buffer, c, tile_rows(zt, d), :],
                    )
                    store(k, i, zt, total)

        def two(n, carry):
            one(start + 2 * n, 0)
            one(start + 2 * n + 1, 1)
            if after is not None:
                after(n)
            return carry

        for n in range((stop - start) // 2):
            two(n, 0)

    def first_main(k, i, zt, total):
        trial[k, i, tile_rows(zt), :] = total

    def second_main(k, i, zt, total):
        state[k, i, tile_rows(zt), :] = 0.5 * state[k, i, tile_rows(zt), :] + 0.005 * total

    def last_main(k, i, zt, total):
        out[k - GROUP, i, 8 * zt : 8 * zt + 8, :] = 0.5 * state[k, i, tile_rows(zt), :] + 0.005 * total

    def first_strip(side, i, zt, total):
        strip_trial[side, i, tile_rows(zt), :] = total

    def second_strip(side, i, zt, total):
        strip[side, i, tile_rows(zt), :] = 0.5 * strip[side, i, tile_rows(zt), :] + 0.005 * total

    strips_eval(strip, first_strip)
    for load in field_loads:
        load.wait()
    main_eval(state, 1, 11, first_main)
    strips_eval(strip_trial, second_strip)
    main_eval(trial, 2, 10, second_main)
    strips_eval(strip, first_strip)
    main_eval(state, 3, 9, first_main)
    strips_eval(strip_trial, None)
    def writing(n):
        done = pl.ds(2 * n, 2)
        return pltpu.make_async_copy(out.at[done], out_hbm.at[done], sems.at[n])

    main_eval(trial, 4, 8, last_main, lambda n: writing(n).start())
    for n in range(GROUP // 2):
        writing(n).wait()


VMEM = pl.BlockSpec(memory_space=pltpu.VMEM)
SMEM = pl.BlockSpec(memory_space=pltpu.SMEM)
ANY = pl.BlockSpec(memory_space=pl.ANY)


SMALL = pl.CostEstimate(flops=8, bytes_accessed=8, transcendentals=0)
LONG = pl.CostEstimate(flops=1_000_000_000, bytes_accessed=100_000_000, transcendentals=0)


def shape(*dims):
    return jax.ShapeDtypeStruct(dims, f32)


def small_kernel(kernel, name, out, in_specs, cost=SMALL):
    out_specs = (VMEM,) * len(out) if isinstance(out, tuple) else VMEM
    return pl.pallas_call(kernel, out_shape=out, in_specs=in_specs, out_specs=out_specs, cost_estimate=cost, name=name)


def steps_call(kernel):
    return pl.pallas_call(
        kernel,
        out_shape=shape(GROUP, 6, 32, 128),
        in_specs=[SMEM] + [VMEM] * 6 + [ANY] * 3,
        out_specs=ANY,
        scratch_shapes=[
            pltpu.VMEM((SLOTS, 6, 48, 128), f32),
            pltpu.VMEM((SLOTS, 6, 48, 128), f32),
            pltpu.VMEM((GROUP, 6, 32, 128), f32),
            pltpu.VMEM((2, 6, 48, 128), f32),
            pltpu.VMEM((2, 6, 48, 128), f32),
            pltpu.VMEM((6, 32, 128), f32),
            pltpu.VMEM((9, 32, 128), f32),
            pltpu.VMEM((2, 9, 32, 128), f32),
            pltpu.VMEM((2, 4, 48, 128), f32),
            pltpu.VMEM((2, 4, 48, 128), f32),
            pltpu.VMEM((2, 6, 32, 128), f32),
            pltpu.VMEM((2, 6, 32, 128), f32),
            pltpu.VMEM((2, 6, 32, 128), f32),
            pltpu.VMEM((2, 6, 32, 128), f32),
            pltpu.SemaphoreType.DMA((8,)),
        ],
        compiler_params=pltpu.CompilerParams(vmem_limit_bytes=32 * 1024 * 1024),
        name="heun_steps",
    )


def body(magnetic, velocity_stack, wavenumber, velocity_owner):
    groups, tiles = lax.axis_size("mode"), lax.axis_size("tile")
    me, tile = lax.axis_index("mode"), lax.axis_index("tile")
    modes = groups * GROUP
    away = jnp.bitwise_xor(me, velocity_owner[0])

    def to_pair(x, first):
        pairs = []
        for i in range(first, groups, 2):
            pairs += [(i, (i + 1) % groups), ((i + 1) % groups, i)]
        return lax.ppermute(x, "mode", pairs)

    def across(x, bit):
        return lax.ppermute(x, "mode", [(i, i ^ bit) for i in range(groups)])

    def to_tile(x, first):
        pairs = []
        for i in range(first, tiles, 2):
            pairs += [(i, (i + 1) % tiles), ((i + 1) % tiles, i)]
        return lax.ppermute(x, "tile", pairs)

    bits = []
    while 2 << len(bits) < groups:
        bits.append(2 << len(bits))
    bits.append(1)
    def choose(x, y, bit):
        return jnp.where(jnp.bitwise_and(away, bit) == 0, x, y)

    pair = to_pair(magnetic, 0)
    flow = choose(velocity_stack, across(velocity_stack, bits[0]), bits[0])
    other = to_pair(magnetic, 1)
    info = jnp.stack(
        [
            lax.rem(wavenumber[0] + modes // 2 + modes - GROUP, modes),
            tile,
            jnp.bitwise_and(away, bits[-1]),
            jnp.bitwise_and(me, 1),
        ]
    ).astype(jnp.int32)
    flow, info = lax.optimization_barrier((flow, info))
    edges = small_kernel(pack_kernel, "pack_edges", shape(9, 8, 128), [VMEM] * 2, LONG)(magnetic, flow)

    def beyond(edges):
        near, far = to_tile(edges, 0), to_tile(edges, 1)
        odd = tile % 2 == 1
        left = jnp.where(tile == 0, 0.0, jnp.where(odd, near, far))
        right = jnp.where(tile == tiles - 1, 0.0, jnp.where(odd, far, near))
        return left, right, lax.broadcasted_iota(jnp.int32, edges.shape, edges.ndim - 1) % 8 < 4

    def as_strips(edges, left, right, low):
        return jnp.stack([jnp.where(low, left, edges), jnp.where(low, edges, right)])

    def middle_rounds(flow, edges):
        for bit in bits[1:-2]:
            flow = choose(flow, across(flow, bit), bit)
        flow2 = across(flow, bits[-2])
        left, right, low = beyond(edges)
        strips = as_strips(edges[:6], left[:6], right[:6], low[:6])
        halo = jnp.where(low[6:], left[6:], right[6:])
        for bit in bits[1:-2]:
            halo = choose(halo, across(halo, bit), bit)
        halo2 = across(halo, bits[-2])
        flow, flow2, halo, halo2 = lax.optimization_barrier((flow, flow2, halo, halo2))
        flow, halo = choose(flow, flow2, bits[-2]), choose(halo, halo2, bits[-2])
        return jnp.concatenate([flow.reshape(36, 8, 128), halo]), strips

    def no_rounds(flow, edges):
        return jnp.zeros((39, 8, 128), f32), jnp.zeros((2, 6, 8, 128), f32)

    def neighbours(pair, other):
        edges = small_kernel(pack_fields_kernel, "pack_field_edges", shape(2, 6, 8, 128), [VMEM] * 2)(pair, other)
        near, far = to_tile(edges, 0), to_tile(edges, 1)
        return edges, near, far

    def no_neighbours(pair, other):
        edges = jnp.zeros((2, 6, 8, 128), f32)
        return edges, edges, edges

    flow, strips = lax.cond(velocity_owner[0] >= 0, middle_rounds, no_rounds, flow, edges)
    flow2 = across(flow, 1)
    edges, near, far = lax.cond(velocity_owner[0] < groups, neighbours, no_neighbours, pair, other)
    return steps_call(functools.partial(steps_kernel, modes, tiles))(info, flow, flow2, strips, edges, near, far, magnetic, pair, other)


def solution(mesh):
    placed = (P("mode", None, None, "tile"), P("mode", None, None, "tile"), P("mode"), P())
    return jax.shard_map(
        body, mesh=mesh, in_specs=placed, out_specs=P("mode", None, None, "tile"), check_vma=False
    )
```

```python
import functools

import jax
import jax.numpy as jnp
from jax import lax
from jax.experimental import pallas as pl
from jax.experimental.pallas import tpu as pltpu
from jax.sharding import PartitionSpec as P

inner_radius = 32.0
f32 = jnp.float32
GROUP = 4
EDGE = 8
SLOTS = 3 * GROUP


def lane_index(rows=8):
    return lax.broadcasted_iota(jnp.int32, (rows, 128), 1)


def turn(x, shift, axis=1):
    if isinstance(shift, int):
        shift %= x.shape[axis]
        if shift == 0:
            return x
    return pltpu.roll(x, shift, axis)


def pack_kernel(field_ref, flow_ref, edges_ref):
    lane = lane_index()
    for comp in range(6):
        total = jnp.zeros((8, 128), f32)
        for zt in range(4):
            for mode in range(GROUP):
                at = 32 * zt + 8 * mode
                piece = turn(field_ref[mode, comp, 8 * zt : 8 * zt + 8, :], at + 4)
                total = jnp.where((lane >= at) & (lane < at + 8), piece, total)
        edges_ref[comp] = total
    for block in range(3):
        total = jnp.zeros((8, 128), f32)
        for part in range(4):
            row = 4 * block + part
            if row < 9:
                for zt in range(4):
                    at = 32 * part + 8 * zt
                    piece = turn(flow_ref[0, row, 8 * zt : 8 * zt + 8, :], at + 4)
                    total = jnp.where((lane >= at) & (lane < at + 8), piece, total)
        edges_ref[6 + block] = total


def pack_fields_kernel(pair_ref, other_ref, edges_ref):
    lane = lane_index()
    for group, field_ref in enumerate((pair_ref, other_ref)):
        for comp in range(6):
            total = jnp.zeros((8, 128), f32)
            for zt in range(4):
                for mode in range(GROUP):
                    at = 32 * zt + 8 * mode
                    piece = turn(field_ref[mode, comp, 8 * zt : 8 * zt + 8, :], at + 4)
                    total = jnp.where((lane >= at) & (lane < at + 8), piece, total)
            edges_ref[group, comp] = total


def emf_of(flow, centre, total, gap):
    steady = flow[0:3]
    swirl_re = (flow[3], flow[5], flow[7])
    swirl_im = (flow[4], flow[6], flow[8])
    out = []
    for comp in range(3):
        i, j = (comp + 1) % 3, (comp + 2) % 3
        real = (
            (steady[i] * centre[2 * j] - steady[j] * centre[2 * i])
            + (swirl_re[i] * total[2 * j] - swirl_re[j] * total[2 * i])
            - (swirl_im[i] * gap[2 * j + 1] - swirl_im[j] * gap[2 * i + 1])
        )
        imag = (
            (steady[i] * centre[2 * j + 1] - steady[j] * centre[2 * i + 1])
            + (swirl_re[i] * total[2 * j + 1] - swirl_re[j] * total[2 * i + 1])
            + (swirl_im[i] * gap[2 * j] - swirl_im[j] * gap[2 * i])
        )
        out += [real, imag]
    return out


def coefficients(radius):
    inner, outer = radius - 1.0, radius + 1.0
    return dict(
        up=1.0 + 0.5 / inner, down=1.0 - 0.5 / outer, flux_up=radius / inner, flux_down=radius / outer,
        inv=1.0 / radius, inv2=1.0 / (radius * radius),
    )


def with_waves(coef, waves):
    return dict(
        coef, waves=waves, decay=6.0 - (waves * waves + 1.0) * coef["inv2"], axial=6.0 - (waves * waves) * coef["inv2"],
        coupling=(2.0 * waves) * coef["inv2"], over=(2.0 * waves) * coef["inv"],
    )


def stencil(field, emf, coef):
    up, down, decay, axial, coupling, over = (coef[n] for n in ("up", "down", "decay", "axial", "coupling", "over"))
    right = [field[i] * up for i in range(6)]
    left = [field[i] * down for i in range(6)]
    place = [field[i] * (decay if i < 4 else axial) for i in range(6)]
    for part in range(2):
        right[2 + part] = right[2 + part] - emf[4 + part]
        left[2 + part] = left[2 + part] + emf[4 + part]
        right[4 + part] = right[4 + part] + emf[2 + part] * coef["flux_up"]
        left[4 + part] = left[4 + part] - emf[2 + part] * coef["flux_down"]
    place[0] = place[0] + (coupling * field[3] - over * emf[5])
    place[1] = place[1] - (coupling * field[2] - over * emf[4])
    place[2] = place[2] - coupling * field[1]
    place[3] = place[3] + coupling * field[0]
    place[4] = place[4] + over * emf[1]
    place[5] = place[5] - over * emf[0]
    return right, left, place


PAD = 8


def tile_rows(zt, shift=0):
    return pl.ds(PAD + 8 * zt + shift, 8)


def add_rows(total, i, get_field, get_emf):
    total = total + (get_field(i, 1) + get_field(i, -1))
    if i < 2:
        total = total - (get_emf(2 + i, 1) - get_emf(2 + i, -1))
    elif i < 4:
        total = total + (get_emf(i - 2, 1) - get_emf(i - 2, -1))
    return total


def wave_at(base, slot, modes):
    return (lax.rem(base + slot, modes) - modes // 2).astype(f32)


def column_radius(column):
    return inner_radius + 0.5 + column.astype(f32)


def steps_kernel(
    modes, tiles, info_ref, flow_ref, flow2_ref, strips_ref, edges_ref, near_ref, far_ref, own_hbm, pair_hbm, other_hbm, out_hbm,
    state, trial, out, strip, strip_trial, inject, flow, flow_strip, emfs, emfs_strip, sums, gaps, rights, lefts, sems,
):
    base, tile, take, odd = info_ref[0], info_ref[1], info_ref[2], info_ref[3]

    places = (GROUP, 2 * GROUP * (1 - odd), 2 * GROUP * odd)
    rows = pl.ds(PAD, 32)
    field_loads = [
        pltpu.make_async_copy(src, state.at[pl.ds(place, GROUP), :, rows], sems.at[4 + i])
        for i, (src, place) in enumerate(zip((own_hbm, pair_hbm, other_hbm), places))
    ]
    for load in field_loads:
        load.start()

    lane8 = lane_index()
    column8 = lane8 % 8
    zeros = jnp.zeros((8, 128), f32)
    for array, slots in ((state, range(1, 11)), (trial, range(2, 10))):
        for k in slots:
            for i in range(6):
                array[k, i, 0:PAD, :] = zeros
                array[k, i, PAD + 32 : PAD + 40, :] = zeros
    for array in (strip, strip_trial, emfs_strip, emfs):
        for side in range(2):
            for i in range(array.shape[1]):
                array[side, i, 0:PAD, :] = zeros
                array[side, i, PAD + 32 : PAD + 40, :] = zeros

    first_column = tile * 128
    main_coef = coefficients(column_radius(first_column + lane8))
    strip_coef, strip_inside = [], []
    for side in range(2):
        column = first_column + column8 + (124 if side else -4)
        strip_coef.append(with_waves(coefficients(column_radius(column)), wave_at(base, lane8 // 8, modes)))
        strip_inside.append((column >= 0) & (column < tiles * 128))

    tile_odd = lax.rem(tile, 2) == 1
    for comp in range(6):
        sides = []
        for group in range(2):
            edges, near, far = edges_ref[group, comp], near_ref[group, comp], far_ref[group, comp]
            left = jnp.where(tile == 0, 0.0, jnp.where(tile_odd, near, far))
            right = jnp.where(tile == tiles - 1, 0.0, jnp.where(tile_odd, far, near))
            sides.append((jnp.where(column8 < 4, left, edges), jnp.where(column8 < 4, edges, right)))
        for side in range(2):
            own, pair, other = strips_ref[side, comp], sides[0][side], sides[1][side]
            low, high = jnp.where(odd == 1, pair, other), jnp.where(odd == 1, other, pair)
            for zt in range(4):
                value = jnp.where(lane8 < 32, turn(low, -32 * zt), turn(own, 32 - 32 * zt))
                value = jnp.where(lane8 < 64, value, turn(high, 64 - 32 * zt))
                strip[side, comp, tile_rows(zt), :] = jnp.where(lane8 < 96, value, 0.0)

    near = jnp.where(column8 < 4, 124 + column8, column8 - 4)
    halos = [jnp.where(take == 0, flow_ref[36 + block], flow2_ref[36 + block]) for block in range(3)]
    for r in range(9):
        for zt in range(4):
            at = slice(8 * zt, 8 * zt + 8)
            value = jnp.where(take == 0, flow_ref[4 * r + zt], flow2_ref[4 * r + zt])
            flow[r, at] = value
            inside = jnp.take_along_axis(value, near, axis=1)
            outside = jnp.take_along_axis(halos[r // 4], 32 * (r % 4) + 8 * zt + column8, axis=1)
            flow_strip[0, r, at] = jnp.where(column8 < 4, outside, inside)
            flow_strip[1, r, at] = jnp.where(column8 < 4, inside, outside)

    def strips_eval(source, store):
        places = [(side, zt) for side in range(2) for zt in range(4)]
        for side, zt in places:
            at = slice(8 * zt, 8 * zt + 8)
            for i in range(6):
                x = source[side, i, tile_rows(zt), :]
                lower, upper = turn(x, EDGE), turn(x, -EDGE)
                sums[side, i, at], gaps[side, i, at] = lower + upper, lower - upper
        terms = {}
        for side, zt in places:
            at = slice(8 * zt, 8 * zt + 8)
            centre = [source[side, i, tile_rows(zt), :] for i in range(6)]
            velocity = [flow_strip[side, r, at, :] for r in range(9)]
            emf = emf_of(velocity, centre, [sums[side, i, at] for i in range(6)], [gaps[side, i, at] for i in range(6)])
            right, left, terms[side, zt] = stencil(centre, emf, strip_coef[side])
            if store is not None:
                for i in range(4):
                    emfs_strip[side, i, tile_rows(zt), :] = emf[i]
            for i in range(6):
                if store is not None or side:
                    rights[side, i, at] = right[i]
                if store is not None or not side:
                    lefts[side, i, at] = left[i]
        for side, zt in places:
            at = slice(8 * zt, 8 * zt + 8)
            for i in range(6):
                if store is not None or side:
                    next_column = turn(rights[side, i, at], -1)
                if store is not None or not side:
                    last_column = turn(lefts[side, i, at], 1)
                inject[i, at] = jnp.where(column8 == 3, next_column, inject[i, at]) if side else last_column
                if store is not None:
                    total = add_rows(
                        (next_column + last_column) + terms[side, zt][i], i,
                        lambda c, d: source[side, c, tile_rows(zt, d), :],
                        lambda c, d: emfs_strip[side, c, tile_rows(zt, d), :],
                    )
                    store(side, i, zt, jnp.where(strip_inside[side], total, 0.0))

    def main_eval(source, start, stop, store, after=None):
        def one(k, buffer):
            coef = with_waves(main_coef, wave_at(base, k, modes))
            totals = []
            for zt in range(4):
                centre = [source[k, i, tile_rows(zt), :] for i in range(6)]
                lower = [source[k - 1, i, tile_rows(zt), :] for i in range(6)]
                upper = [source[k + 1, i, tile_rows(zt), :] for i in range(6)]
                total = [lower[i] + upper[i] for i in range(6)]
                gap = [lower[i] - upper[i] for i in range(6)]
                emf = emf_of([flow[r, 8 * zt : 8 * zt + 8, :] for r in range(9)], centre, total, gap)
                for i in range(4):
                    emfs[buffer, i, tile_rows(zt), :] = emf[i]
                right, left, place = stencil(centre, emf, coef)
                total = []
                for i in range(6):
                    edge = pltpu.roll(inject[i, 8 * zt : 8 * zt + 8, :], 124 - EDGE * k, 1)
                    next_column = jnp.where(lane8 == 127, edge, turn(right[i], -1))
                    last_column = jnp.where(lane8 == 0, edge, turn(left[i], 1))
                    total.append((next_column + last_column) + place[i])
                totals.append(total)
            for zt in range(4):
                for i in range(6):
                    total = add_rows(
                        totals[zt][i], i,
                        lambda c, d: source[k, c, tile_rows(zt, d), :],
                        lambda c, d: emfs[buffer, c, tile_rows(zt, d), :],
                    )
                    store(k, i, zt, total)

        def two(n, carry):
            for m in range(2):
                one(start + 2 * n + m, m)
                if after is not None:
                    after(2 * n + m)
            return carry

        for n in range((stop - start) // 2):
            two(n, 0)

    def first_main(k, i, zt, total):
        trial[k, i, tile_rows(zt), :] = total

    def second_main(k, i, zt, total):
        state[k, i, tile_rows(zt), :] = 0.5 * state[k, i, tile_rows(zt), :] + 0.005 * total

    def last_main(k, i, zt, total):
        out[k - GROUP, i, 8 * zt : 8 * zt + 8, :] = 0.5 * state[k, i, tile_rows(zt), :] + 0.005 * total

    def first_strip(side, i, zt, total):
        strip_trial[side, i, tile_rows(zt), :] = total

    def second_strip(side, i, zt, total):
        strip[side, i, tile_rows(zt), :] = 0.5 * strip[side, i, tile_rows(zt), :] + 0.005 * total

    strips_eval(strip, first_strip)
    for load in field_loads:
        load.wait()
    main_eval(state, 1, 11, first_main)
    strips_eval(strip_trial, second_strip)
    main_eval(trial, 2, 10, second_main)
    strips_eval(strip, first_strip)
    main_eval(state, 3, 9, first_main)
    strips_eval(strip_trial, None)
    def writing(n):
        done = pl.ds(n, 1)
        return pltpu.make_async_copy(out.at[done], out_hbm.at[done], sems.at[n])

    main_eval(trial, 4, 8, last_main, lambda n: writing(n).start())
    for n in range(GROUP):
        writing(n).wait()


VMEM = pl.BlockSpec(memory_space=pltpu.VMEM)
SMEM = pl.BlockSpec(memory_space=pltpu.SMEM)
ANY = pl.BlockSpec(memory_space=pl.ANY)


SMALL = pl.CostEstimate(flops=8, bytes_accessed=8, transcendentals=0)
LONG = pl.CostEstimate(flops=1_000_000_000, bytes_accessed=100_000_000, transcendentals=0)


def shape(*dims):
    return jax.ShapeDtypeStruct(dims, f32)


def small_kernel(kernel, name, out, in_specs, cost=SMALL):
    out_specs = (VMEM,) * len(out) if isinstance(out, tuple) else VMEM
    return pl.pallas_call(kernel, out_shape=out, in_specs=in_specs, out_specs=out_specs, cost_estimate=cost, name=name)


def steps_call(kernel):
    return pl.pallas_call(
        kernel,
        out_shape=shape(GROUP, 6, 32, 128),
        in_specs=[SMEM] + [VMEM] * 6 + [ANY] * 3,
        out_specs=ANY,
        scratch_shapes=[
            pltpu.VMEM((SLOTS, 6, 48, 128), f32),
            pltpu.VMEM((SLOTS, 6, 48, 128), f32),
            pltpu.VMEM((GROUP, 6, 32, 128), f32),
            pltpu.VMEM((2, 6, 48, 128), f32),
            pltpu.VMEM((2, 6, 48, 128), f32),
            pltpu.VMEM((6, 32, 128), f32),
            pltpu.VMEM((9, 32, 128), f32),
            pltpu.VMEM((2, 9, 32, 128), f32),
            pltpu.VMEM((2, 4, 48, 128), f32),
            pltpu.VMEM((2, 4, 48, 128), f32),
            pltpu.VMEM((2, 6, 32, 128), f32),
            pltpu.VMEM((2, 6, 32, 128), f32),
            pltpu.VMEM((2, 6, 32, 128), f32),
            pltpu.VMEM((2, 6, 32, 128), f32),
            pltpu.SemaphoreType.DMA((8,)),
        ],
        compiler_params=pltpu.CompilerParams(vmem_limit_bytes=32 * 1024 * 1024),
        name="heun_steps",
    )


def body(magnetic, velocity_stack, wavenumber, velocity_owner):
    groups, tiles = lax.axis_size("mode"), lax.axis_size("tile")
    me, tile = lax.axis_index("mode"), lax.axis_index("tile")
    modes = groups * GROUP
    away = jnp.bitwise_xor(me, velocity_owner[0])

    def to_pair(x, first):
        pairs = []
        for i in range(first, groups, 2):
            pairs += [(i, (i + 1) % groups), ((i + 1) % groups, i)]
        return lax.ppermute(x, "mode", pairs)

    def across(x, bit):
        return lax.ppermute(x, "mode", [(i, i ^ bit) for i in range(groups)])

    def to_tile(x, first):
        pairs = []
        for i in range(first, tiles, 2):
            pairs += [(i, (i + 1) % tiles), ((i + 1) % tiles, i)]
        return lax.ppermute(x, "tile", pairs)

    bits = []
    while 2 << len(bits) < groups:
        bits.append(2 << len(bits))
    bits.append(1)
    def choose(x, y, bit):
        return jnp.where(jnp.bitwise_and(away, bit) == 0, x, y)

    pair = to_pair(magnetic, 0)
    flow = choose(velocity_stack, across(velocity_stack, bits[0]), bits[0])
    other = to_pair(magnetic, 1)
    info = jnp.stack(
        [
            lax.rem(wavenumber[0] + modes // 2 + modes - GROUP, modes),
            tile,
            jnp.bitwise_and(away, bits[-1]),
            jnp.bitwise_and(me, 1),
        ]
    ).astype(jnp.int32)
    flow, info = lax.optimization_barrier((flow, info))
    edges = small_kernel(pack_kernel, "pack_edges", shape(9, 8, 128), [VMEM] * 2, LONG)(magnetic, flow)

    def beyond(edges):
        near, far = to_tile(edges, 0), to_tile(edges, 1)
        odd = tile % 2 == 1
        left = jnp.where(tile == 0, 0.0, jnp.where(odd, near, far))
        right = jnp.where(tile == tiles - 1, 0.0, jnp.where(odd, far, near))
        return left, right, lax.broadcasted_iota(jnp.int32, edges.shape, edges.ndim - 1) % 8 < 4

    def as_strips(edges, left, right, low):
        return jnp.stack([jnp.where(low, left, edges), jnp.where(low, edges, right)])

    def middle_rounds(flow, edges):
        for bit in bits[1:-2]:
            flow = choose(flow, across(flow, bit), bit)
        flow2 = across(flow, bits[-2])
        left, right, low = beyond(edges)
        strips = as_strips(edges[:6], left[:6], right[:6], low[:6])
        halo = jnp.where(low[6:], left[6:], right[6:])
        for bit in bits[1:-2]:
            halo = choose(halo, across(halo, bit), bit)
        halo2 = across(halo, bits[-2])
        flow, flow2, halo, halo2 = lax.optimization_barrier((flow, flow2, halo, halo2))
        flow, halo = choose(flow, flow2, bits[-2]), choose(halo, halo2, bits[-2])
        return jnp.concatenate([flow.reshape(36, 8, 128), halo]), strips

    def no_rounds(flow, edges):
        return jnp.zeros((39, 8, 128), f32), jnp.zeros((2, 6, 8, 128), f32)

    def neighbours(pair, other):
        edges = small_kernel(pack_fields_kernel, "pack_field_edges", shape(2, 6, 8, 128), [VMEM] * 2)(pair, other)
        near, far = to_tile(edges, 0), to_tile(edges, 1)
        return edges, near, far

    def no_neighbours(pair, other):
        edges = jnp.zeros((2, 6, 8, 128), f32)
        return edges, edges, edges

    flow, strips = lax.cond(velocity_owner[0] >= 0, middle_rounds, no_rounds, flow, edges)
    flow2 = across(flow, 1)
    edges, near, far = lax.cond(velocity_owner[0] < groups, neighbours, no_neighbours, pair, other)
    return steps_call(functools.partial(steps_kernel, modes, tiles))(info, flow, flow2, strips, edges, near, far, magnetic, pair, other)


def solution(mesh):
    placed = (P("mode", None, None, "tile"), P("mode", None, None, "tile"), P("mode"), P())
    return jax.shard_map(
        body, mesh=mesh, in_specs=placed, out_specs=P("mode", None, None, "tile"), check_vma=False
    )
```
